128 devices in a mesh: fsdp: 8 (over y, x_lo), context: 16 (over z, x_hi, core).
Axes of the slice: x: 4 (x_hi: 2, x_lo: 2; x = x_hi * 2 + x_lo), y: 4, z: 4, core: 2. Of those that a mesh axis runs over, the one named last changes fastest.
Arguments:
- hidden: bfloat16 [16384, 2048], P(('fsdp', 'context')), may hold values from -6 to 6
- cotangent: bfloat16 [16384, 2048], P(('fsdp', 'context')), may hold values from -6 to 6
- lengths: int32 [8, 4], P('fsdp'), may hold values from 1 to 1536, 2048 in all within a row
- source_pos: int32 [8, 2048], P('fsdp'), may hold values from 0 to 2047, as said below
- owner_slot: int32 [8, 2048], P('fsdp'), may hold values from 0 to 2047, as said below
- ln1_gain: bfloat16 [2048], P('fsdp'), may hold values from 0.099609375 to 1.8984375
- ln1_bias: bfloat16 [2048], P('fsdp'), may hold values from -4 to 4
- query_weight: bfloat16 [2048, 2048], P('fsdp'), may hold values from -1 to 1
- query_bias: bfloat16 [2048], P('fsdp'), may hold values from -4 to 4
- kv_weight: bfloat16 [2048, 256], P('fsdp'), may hold values from -0.125 to 0.125
- value_bias: bfloat16 [128], P('fsdp'), may hold values from -4 to 4
- out_weight: bfloat16 [2048, 2048], P('fsdp'), may hold values from -0.25 to 0.25
- out_bias: bfloat16 [2048], P('fsdp'), may hold values from -4 to 4
- ln2_gain: bfloat16 [2048], P('fsdp'), may hold values from 0.099609375 to 1.8984375
- ln2_bias: bfloat16 [2048], P('fsdp'), may hold values from -4 to 4
- fc_weight: bfloat16 [2048, 8192], P('fsdp'), may hold values from -0.125 to 0.125
- fc_bias: bfloat16 [8192], P('fsdp'), may hold values from -4 to 4
- proj_weight: bfloat16 [8192, 2048], P('fsdp'), may hold values from -0.09375 to 0.09375
- proj_bias: bfloat16 [2048], P('fsdp'), may hold values from -4 to 4
Outputs:
- output: bfloat16 [16384, 2048], P(('fsdp', 'context'))
- grad_hidden: bfloat16 [16384, 2048], P(('fsdp', 'context'))
- grad_ln1_gain: float32 [2048], P('fsdp')
- grad_ln1_bias: float32 [2048], P('fsdp')
- grad_query_weight: float32 [2048, 2048], P('fsdp')
- grad_query_bias: float32 [2048], P('fsdp')
- grad_kv_weight: float32 [2048, 256], P('fsdp')
- grad_value_bias: float32 [128], P('fsdp')
- grad_out_weight: float32 [2048, 2048], P('fsdp')
- grad_out_bias: float32 [2048], P('fsdp')
- grad_ln2_gain: float32 [2048], P('fsdp')
- grad_ln2_bias: float32 [2048], P('fsdp')
- grad_fc_weight: float32 [2048, 8192], P('fsdp')
- grad_fc_bias: float32 [8192], P('fsdp')
- grad_proj_weight: float32 [8192, 2048], P('fsdp')
- grad_proj_bias: float32 [2048], P('fsdp')
- maxima: float32 [16], replicated
- clipped_query_weight: float32 [2048, 2048], P('fsdp')
- clipped_query_bias: float32 [2048], P('fsdp')
- clipped_key_weight: float32 [2048, 128], P('fsdp')
The draws below stay inside these ranges and needn't reach their ends.
Inputs may be any that keep to these rules, and one draw needn't show every extreme that they name: `lengths`: each row sums to 2048; its largest entry is 1536. In each batch owner_slot is a permutation; slot s lies on the device s // 128 of the context axis, in its row s % 128; the tokens of natural positions c * 128 to (c + 1) * 128 - 1 fill the rows c * 8 to (c + 1) * 8 - 1 of every device of the context axis. `source_pos`: in each batch the inverse permutation of owner_slot.
All inputs are finite; a program needn't handle non-finite values.
Results may differ from the reference program's by a relative error of at most 0.025.
Values may be sent and summed in bfloat16 or wider, within the bound.
No kernel may reach another device: no remote copies, remote signals or barrier semaphores. Data moves between devices by JAX's collectives and lax.ppermute only.
A program may use at most 512 MiB of HBM per device.

```python
import math
import jax
import jax.numpy as jnp
import numpy as np
from jax import lax

D = 2048
HEADS = 16
HD = 128
FF = 8192
SEQS = 4
ROWS = 128
GROUP = 2048
SUB = 8
MOST = 1536
TOKENS = 16384
N_FSDP = 8


def slot_table(key):
    key = jax.random.fold_in(key, 11)
    devices_ctx = GROUP // ROWS
    keys = jax.random.split(key, N_FSDP * devices_ctx)
    orders = jax.vmap(lambda part_key: jax.random.permutation(part_key, ROWS))(keys).astype(jnp.int32)
    source_dev = jnp.tile(jnp.arange(devices_ctx, dtype=jnp.int32), N_FSDP)[:, None]
    slots = orders // SUB * ROWS + source_dev * SUB + orders % SUB
    return slots.reshape(N_FSDP, GROUP).astype(jnp.int32)


def draw_owner_slot(key, part):
    return slot_table(key)


def draw_source_pos(key, part):
    return jnp.argsort(slot_table(key), axis=1).astype(jnp.int32)


def draw_query_weight(key, part):
    key = jax.random.fold_in(key, 5)
    scale_key, entry_key = jax.random.split(key)
    head_scale = jnp.exp(jax.random.uniform(scale_key, (HEADS,), jnp.float32, 0.0, math.log(3.0)))
    entries = jnp.clip(jax.random.normal(entry_key, (D, D), jnp.float32), -4.0, 4.0) / math.sqrt(D)
    return (entries * jnp.repeat(head_scale, HD)[None, :]).astype(jnp.bfloat16)


def block_levels(stream_key, extent, pieces, low, largest):
    factor_of = 1.0
    for dim, blocks in pieces:
        heights = jax.random.uniform(jax.random.fold_in(jax.random.fold_in(stream_key, 6), dim), (blocks,), jnp.float32, low / len(pieces), largest / len(pieces))
        factor_of = factor_of * jnp.repeat(jnp.exp(heights), extent[dim] // blocks).reshape((-1,) + (1,) * (len(extent) - 1 - dim))
    return factor_of


def profile(number_of, total, most, slope):
    portions = [(1 << 20) // math.isqrt(grade ** slope) + 1 for grade in range(2, number_of + 1)]
    spare, counts = total - most - (number_of - 1), [1] * (number_of - 1)
    while spare > 0:
        free = [i for i in range(number_of - 1) if counts[i] < most]
        whole, remaining = sum([portions[i] for i in free]), spare
        for i in free:
            extra = min(most - counts[i], max(1, remaining * portions[i] // whole), spare)
            counts[i] = counts[i] + extra
            spare = spare - extra
    return np.array([most] + counts)


def ragged(key, amount, total, reach, lean):
    if amount == 2:
        one = jax.random.randint(key, (), max(1, total - reach), min(reach, total - 1) + 1)
        return jnp.stack([one, total - one])
    sizes = jnp.asarray(profile(amount, total, reach, lean), jnp.int32)
    twos = (amount - 1) // 2
    source_of, sink = sizes[1:1 + 2 * twos:2], sizes[2:2 + 2 * twos:2]
    room = jnp.minimum(source_of - 1, reach - sink)
    passed = jax.random.randint(jax.random.fold_in(key, 1), (twos,), 0, 1 << 20) % (room + 1)
    sizes = sizes.at[1:1 + 2 * twos:2].set(source_of - passed).at[2:2 + 2 * twos:2].set(sink + passed)
    return sizes[jax.random.permutation(jax.random.fold_in(key, 2), amount)]


def gaussian(key, shape, deviation, limit, shards=(), kind=jnp.bfloat16):
    array = jax.random.normal(key, shape, jnp.float32) * deviation
    if len(shards) > 0:
        array = block_levels(key, shape, shards, -0.22, 0.18) * array
    return jnp.clip(array, min=-limit, max=limit).astype(kind)


def setup_inputs(seed: int = 0) -> dict:
    streams_of = jax.random.split(jax.random.key(seed), 20)
    return {
        "hidden": gaussian(streams_of[0], (TOKENS, D), 1.0, 6.0, ((0, 128),)),
        "cotangent": gaussian(streams_of[1], (TOKENS, D), 1.0, 6.0, ((0, 128),)),
        "lengths": jax.vmap(lambda own: ragged(own, SEQS, GROUP, MOST, 1))(jax.random.split(streams_of[2], N_FSDP)).reshape((N_FSDP, SEQS)).astype(jnp.int32),
        "source_pos": draw_source_pos(jax.random.fold_in(streams_of[19], 71), 0),
        "owner_slot": draw_owner_slot(jax.random.fold_in(streams_of[19], 71), 0),
        "ln1_gain": jnp.clip(1.0 + 0.18 * jax.random.normal(streams_of[5], (D,), jnp.float32), 0.099609375, 1.8984375).astype(jnp.bfloat16),
        "ln1_bias": gaussian(streams_of[6], (D,), 0.3, 4.0, ((0, 8),)),
        "query_weight": draw_query_weight(jax.random.fold_in(streams_of[19], 71), 0),
        "query_bias": gaussian(streams_of[8], (D,), 0.3, 4.0, ((0, 8),)),
        "kv_weight": gaussian(streams_of[9], (D, 2 * HD), D ** -0.5, 0.125, ((0, 8),)),
        "value_bias": gaussian(streams_of[10], (HD,), 0.3, 4.0, ((0, 8),)),
        "out_weight": gaussian(streams_of[11], (D, D), (D // 4) ** -0.5, 0.25, ((0, 8),)),
        "out_bias": gaussian(streams_of[12], (D,), 0.3, 4.0, ((0, 8),)),
        "ln2_gain": jnp.clip(1.0 + 0.18 * jax.random.normal(streams_of[13], (D,), jnp.float32), 0.099609375, 1.8984375).astype(jnp.bfloat16),
        "ln2_bias": gaussian(streams_of[14], (D,), 0.3, 4.0, ((0, 8),)),
        "fc_weight": gaussian(streams_of[15], (D, FF), D ** -0.5, 0.125, ((0, 8),)),
        "fc_bias": gaussian(streams_of[16], (FF,), 0.3, 4.0, ((0, 8),)),
        "proj_weight": gaussian(streams_of[17], (FF, D), (FF // 2) ** -0.5, 0.09375, ((0, 8),)),
        "proj_bias": gaussian(streams_of[18], (D,), 0.3, 4.0, ((0, 8),)),
    }


EPSILON = 1e-05
CLIP_LIMIT = 4.0
MASKED = -1e+30

@jax.custom_vjp
def low(v):
    return lax.optimization_barrier(v.astype(jnp.bfloat16)).astype(jnp.float32)

@jax.custom_vjp
def low_back(v):
    return v

def low_keep(v):
    return (low(v), None)

def low_pass(kept, grad):
    return (grad,)

def back_keep(v):
    return (v, None)

def back_low(kept, grad):
    return (low(grad),)
low.defvjp(low_keep, low_pass)
low_back.defvjp(back_keep, back_low)

def layer_norm(values, norm_gain, norm_shift):
    centered = values - lax.optimization_barrier(jnp.mean(values, axis=-1, keepdims=True))
    spread = lax.optimization_barrier(jnp.mean(centered * centered, axis=-1, keepdims=True))
    return centered * lax.rsqrt(spread + EPSILON) * norm_gain + norm_shift

def product(left_side, right_side):
    return jnp.dot(left_side, right_side, preferred_element_type=jnp.float32, precision=lax.Precision.HIGHEST)

def allowed_pairs(seq_lengths, positions):
    seq_ends = jnp.cumsum(seq_lengths).astype(jnp.int32)
    starts = (seq_ends - seq_lengths).astype(jnp.int32)
    seq_start = lax.optimization_barrier(jnp.max(jnp.where(starts[None, :] <= positions[:, None], starts[None, :], 0), axis=1))
    return (positions[None, :] <= positions[:, None]) & (positions[None, :] >= seq_start[:, None])

def layer_forward(inputs, params, allowed):
    gain_one, shift_one, w_query, b_query, w_kv, b_value, w_out, b_out, gain_two, shift_two, w_fc, b_fc, w_proj, b_proj = params
    normed_one = low(layer_norm(inputs, gain_one, shift_one))
    queries = low(low_back(product(normed_one, w_query) + b_query))
    kv_shift = jnp.concatenate([jnp.zeros((HD,), jnp.float32), b_value])
    key_value = low(low_back(product(normed_one, w_kv) + kv_shift))
    all_keys = key_value[:, :HD]
    all_values = key_value[:, HD:]
    query_heads = queries.reshape(GROUP, HEADS, HD)
    scores = jnp.einsum('shd,td->hst', query_heads, all_keys, precision=lax.Precision.HIGHEST)
    scores = low_back(scores * (1.0 / math.sqrt(HD)))
    masked = jnp.where(allowed[None, :, :], scores, MASKED)
    head_max = lax.optimization_barrier(jnp.max(masked, axis=(1, 2)))
    row_max = lax.optimization_barrier(jnp.max(masked, axis=2, keepdims=True))
    weights_exp = jnp.exp(masked - row_max)
    probs_now = weights_exp / lax.optimization_barrier(jnp.sum(weights_exp, axis=2, keepdims=True))
    attended = jnp.einsum('hst,td->shd', low(probs_now), all_values, precision=lax.Precision.HIGHEST)
    attended = low(low_back(attended.reshape(GROUP, D)))
    after_attn = inputs + low_back(product(attended, w_out) + b_out)
    normed_two = low(layer_norm(after_attn, gain_two, shift_two))
    pre_act = low_back(product(normed_two, w_fc) + b_fc)
    activated = low(jax.nn.gelu(pre_act, approximate=True))
    return (after_attn + low_back(product(activated, w_proj) + b_proj), head_max)

def add_up(running_sum, new_term):
    return running_sum + new_term

def reference(hidden, cotangent, lengths, source_pos, owner_slot, ln1_gain, ln1_bias, query_weight, query_bias, kv_weight, value_bias, out_weight, out_bias, ln2_gain, ln2_bias, fc_weight, fc_bias, proj_weight, proj_bias):
    params = tuple((weight.astype(jnp.float32) for weight in (ln1_gain, ln1_bias, query_weight, query_bias, kv_weight, value_bias, out_weight, out_bias, ln2_gain, ln2_bias, fc_weight, fc_bias, proj_weight, proj_bias)))
    grouped = (hidden.reshape(N_FSDP, GROUP, D), cotangent.reshape(N_FSDP, GROUP, D), lengths, source_pos, owner_slot)

    def one_group(carry, inputs):
        token_rows, cot_rows, seq_lengths, positions, slots = inputs
        allowed = allowed_pairs(seq_lengths, positions)

        def forward(values, weights):
            return layer_forward(values, weights, allowed)
        result, pullback, head_max = jax.vjp(forward, token_rows.astype(jnp.float32), params, has_aux=True)
        natural = result[slots]
        dealt_rows = jnp.zeros((GROUP, D), jnp.float32).at[slots].set(cot_rows.astype(jnp.float32))
        grad_rows, grad_params = pullback(dealt_rows)
        sums, running = carry
        sums = jax.tree.map(add_up, sums, grad_params)
        return ((sums, jnp.maximum(running, head_max)), (natural.astype(jnp.bfloat16), grad_rows.astype(jnp.bfloat16)))
    initial = (jax.tree.map(jnp.zeros_like, params), jnp.full((HEADS,), MASKED, jnp.float32))
    (sums, maxima), (outputs, grad_rows) = lax.scan(one_group, initial, grouped)
    clip_ratio = CLIP_LIMIT / jnp.maximum(maxima, CLIP_LIMIT)
    column_scale = jnp.repeat(jnp.sqrt(clip_ratio), HD)
    clipped_qw = params[2] * column_scale[None, :]
    clipped_qb = params[3] * column_scale
    clipped_kw = params[4][:, :HD] * jnp.sqrt(jnp.min(clip_ratio))
    return (outputs.reshape(TOKENS, D), grad_rows.reshape(TOKENS, D), sums[0], sums[1], sums[2], sums[3], sums[4], sums[5], sums[6], sums[7], sums[8], sums[9], sums[10], sums[11], sums[12], sums[13], maxima, clipped_qw, clipped_qb, clipped_kw)
```

```python
import functools
import math

import jax
import jax.numpy as jnp
from jax import lax
from jax.experimental import pallas as pl
from jax.experimental.pallas import tpu as pltpu
from jax.sharding import Mesh
from jax.sharding import PartitionSpec as P

Y, XL, Z, XH, CORE = ("fsdp_0", "fsdp_1", "context_0", "context_1", "context_2")
FSDP = (Y, XL)
CONTEXT = (Z, XH, CORE)
ZX = (Z, XH)
EVERY = (Y, XL, Z, XH, CORE)

EPSILON = 1e-05
CLIP_LIMIT = 4.0
MASKED = -1e30
LANES = 128
BF = jnp.bfloat16
F32 = jnp.float32


def shift(array, axis, by):
    n = lax.axis_size(axis)
    return lax.ppermute(array, axis, [(i, (i + by) % n) for i in range(n)])


def swap(array, axis):
    return shift(array, axis, 1)


def copies(array, axis):
    n = lax.axis_size(axis)
    return lax.all_to_all(jnp.broadcast_to(array[None], (n, *array.shape)), axis, 0, 0, tiled=True)


def pick(array, index, dim):
    return lax.dynamic_index_in_dim(array, index, dim, keepdims=False)


def pair(own, other, index):
    return jnp.where(index == 0, jnp.stack([own, other]), jnp.stack([other, own]))


def assemble(pieces, rows):
    arrays = [a.reshape(-1, a.shape[-1]) for a, _ in pieces]
    width = arrays[0].shape[1]
    counts = [a.shape[0] // LANES for a in arrays]
    firsts = [sum(counts[:k]) for k in range(len(counts))]
    at = [o // LANES for _, offsets in pieces for o in offsets]

    def kernel(at_ref, *refs):
        step, out = pl.program_id(0), refs[-1]
        for source, first, count in zip(refs, firsts, counts):

            @pl.when((step >= first) & (step < first + count))
            def _(source=source):
                out[...] = source[...]

    def block_of(first, count):
        return lambda k, at_ref: (jnp.clip(k - first, 0, count - 1), 0)

    return pl.pallas_call(
        kernel,
        grid_spec=pltpu.PrefetchScalarGridSpec(
            num_scalar_prefetch=1,
            grid=(rows // LANES,),
            in_specs=[
                pl.BlockSpec((LANES, width), block_of(f, n)) for f, n in zip(firsts, counts)
            ],
            out_specs=pl.BlockSpec((LANES, width), lambda k, at_ref: (at_ref[k], 0)),
        ),
        out_shape=jax.ShapeDtypeStruct((rows, width), arrays[0].dtype),
        compiler_params=pltpu.CompilerParams(vmem_limit_bytes=32 * 2**20),
        cost_estimate=pl.CostEstimate(
            flops=0, bytes_accessed=2 * rows * width * 2, transcendentals=0
        ),
        name="assemble",
    )(jnp.stack([jnp.asarray(o, jnp.int32) for o in at]), *arrays)


def matmul(left, right):
    return jnp.dot(left, right, preferred_element_type=F32)


def tall(left, right):
    return lax.dot_general(left, right, (((0,), (0,)), ((), ())), preferred_element_type=F32)


def wide(left, right):
    return lax.dot_general(left, right, (((1,), (1,)), ((), ())), preferred_element_type=F32)


def gelu_tanh(values):
    return jax.nn.gelu(values, approximate=True)


def norm_parts(values):
    centered = values - jnp.mean(values, axis=-1, keepdims=True)
    rate = lax.rsqrt(jnp.mean(centered * centered, axis=-1, keepdims=True) + EPSILON)
    return centered * rate, rate


def norm_back(grad, gain, hat, rate):
    e = grad * gain
    inner = jnp.mean(e * hat, axis=-1, keepdims=True)
    return rate * (e - jnp.mean(e, axis=-1, keepdims=True) - hat * inner)


def shards(
    hidden,
    cotangent,
    lengths,
    source_pos,
    owner_slot,
    ln1_gain,
    ln1_bias,
    query_weight,
    query_bias,
    kv_weight,
    value_bias,
    out_weight,
    out_bias,
    ln2_gain,
    ln2_bias,
    fc_weight,
    fc_bias,
    proj_weight,
    proj_bias,
):
    rows, width = hidden.shape
    ny, nz, nctx = lax.axis_size(Y), lax.axis_size(Z), lax.axis_size(CONTEXT)
    y, xl, z, c = (lax.axis_index(a) for a in (Y, XL, Z, CORE))
    xo, co = 1 - xl, 1 - c
    ctx = lax.axis_index(CONTEXT)
    sub = rows // nctx
    head = kv_weight.shape[1] // 2
    heads = width // head
    scale = 1.0 / math.sqrt(head)
    shard = query_weight.shape[0]
    half = shard // 2
    ff = proj_weight.shape[0]
    block = 2 * ff

    small = jnp.concatenate(
        [
            jnp.stack([ln1_gain, ln1_bias, query_bias, out_bias, ln2_gain, ln2_bias, proj_bias]),
            jnp.pad(value_bias, (0, shard - value_bias.shape[0]))[None],
            fc_bias.reshape(-1, shard),
            jnp.zeros((4, shard), BF),
            kv_weight,
        ]
    )
    small = copies(small, FSDP)
    gain1, bias1, bq, bo, gain2, bias2, bproj = (
        small[:, k].reshape(width).astype(F32) for k in range(7)
    )
    bv = small[:, 7, : value_bias.shape[0]].reshape(head).astype(F32)
    bfc = pick(small[:, 8:12].reshape(ny, block), y, 0).astype(F32)
    wkv = small[:, 16:].reshape(width, 2 * head)

    q_half = lax.dynamic_slice_in_dim(query_weight, half * c, half)
    pieces = [(query_weight, [shard * y, shard * y + half])]
    for d in (1, 3, 2):
        got = shift(q_half, Y, d)
        at = shard * ((y - d) % ny)
        pieces += [(got, [at + half * c]), (swap(got, CORE), [at + half * co])]
    wq = assemble(pieces, ny * shard)

    def gathered(own, halves):
        got = [halves[0]] + [shift(halves[d], Y, d) for d in range(1, ny)]
        mine = jnp.stack(got)
        passed = swap(pick(mine, z, 0), XL)
        theirs = jnp.stack([passed] + [shift(passed, Z, e) for e in range(1, nz)])
        at_mine = [shard * (2 * ((y - d) % ny) + xl) for d in range(ny)]
        at_theirs = [shard * (2 * ((y - (z - e) % nz) % ny) + xo) for e in range(nz)]
        parts = [(own, [at_mine[0], at_mine[0] + half])]
        parts += [(mine[1:], [a + half * c for a in at_mine[1:]])]
        parts += [(swap(mine[1:], CORE), [a + half * co for a in at_mine[1:]])]
        parts += [(theirs, [a + half * c for a in at_theirs])]
        parts += [(swap(theirs, CORE), [a + half * co for a in at_theirs])]
        return assemble(parts, 2 * ny * shard)

    o_half = lax.dynamic_slice_in_dim(out_weight, half * c, half)
    wo = gathered(out_weight, [o_half] * ny)
    wfc = gathered(
        lax.dynamic_slice(fc_weight, (0, block * y), (shard, block)),
        [
            lax.dynamic_slice(fc_weight, (half * c, block * ((y + d) % ny)), (half, block))
            for d in range(ny)
        ],
    )
    passed = swap(
        lax.dynamic_slice(proj_weight, (shard * z + half * c, 0), (half, width)), XL
    )
    theirs = jnp.stack([passed] + [shift(passed, Z, e) for e in range(1, nz)])
    at_theirs = [ff * xo + shard * ((z - e) % nz) for e in range(nz)]
    wproj = assemble(
        [
            (proj_weight, [ff * xl + LANES * k for k in range(ff // LANES)]),
            (theirs, [a + half * c for a in at_theirs]),
            (swap(theirs, CORE), [a + half * co for a in at_theirs]),
        ],
        block,
    )

    x = hidden.astype(F32)
    hat1, rate1 = norm_parts(x)
    h1 = (hat1 * gain1 + bias1).astype(BF)
    kv = matmul(h1, wkv) + jnp.concatenate([jnp.zeros((head,), F32), bv])
    all_kv = copies(kv.astype(BF), CONTEXT).reshape(nctx * rows, 2 * head)
    keys, values = all_kv[:, :head], all_kv[:, head:]
    by_shard = h1.reshape(rows, ny, 2, shard)
    h1_theirs = swap(pick(by_shard, xo, 2).reshape(rows, ny * shard), XL)
    h1_mine = pick(by_shard, xl, 2).reshape(rows, ny * shard)
    q_terms = matmul(jnp.concatenate([h1_mine, h1_theirs]), wq)
    q = (q_terms[:rows] + swap(q_terms[rows:].astype(BF), XL).astype(F32) + bq).astype(BF)

    positions = source_pos[0]
    starts = jnp.cumsum(lengths[0]) - lengths[0]
    own_pos = lax.dynamic_slice_in_dim(positions, ctx * rows, rows)
    seq_start = jnp.max(jnp.where(starts[None, :] <= own_pos[:, None], starts[None, :], 0), axis=1)
    allowed = (positions[None, :] <= own_pos[:, None]) & (positions[None, :] >= seq_start[:, None])
    q_heads = q.reshape(rows, heads, head)

    def score_block():
        raw = jnp.einsum("rhd,kd->rhk", q_heads, keys, preferred_element_type=F32)
        return jnp.where(allowed[:, None, :], raw * scale, MASKED)

    masked = score_block()
    local_max = jnp.max(masked, axis=(0, 2))
    row_max = jnp.max(masked, axis=2, keepdims=True)
    log_total = row_max + jnp.log(jnp.sum(jnp.exp(masked - row_max), axis=2, keepdims=True))
    probs = jnp.exp(masked - log_total).astype(BF)
    attended = jnp.einsum("rhk,kd->rhd", probs, values, preferred_element_type=F32)
    attended = attended.reshape(rows, width).astype(BF)

    x2 = x + matmul(attended, wo) + bo
    hat2, rate2 = norm_parts(x2)
    h2 = (hat2 * gain2 + bias2).astype(BF)

    def over_y(array):
        return jnp.concatenate([array] + [shift(array, Y, d) for d in range(1, ny)])

    def summed_over_y(terms):
        terms = terms.reshape(ny, rows, width)
        got = [shift(terms[d].astype(BF), Y, -d).astype(F32) for d in range(1, ny)]
        return functools.reduce(jnp.add, got, terms[0])

    h2_all = over_y(h2)

    owned = lax.dynamic_slice_in_dim(owner_slot[0], ctx * rows, rows)
    target = owned // rows * sub + owned % rows - ctx * sub
    deal = (target[:, None] == jnp.arange(rows, dtype=jnp.int32)[None, :]).astype(BF)

    def dealt(array):
        pieces = array.reshape(nctx, sub, width)
        return lax.all_to_all(pieces, CONTEXT, 0, 0, tiled=True).reshape(rows, width)

    dy = dealt(tall(deal, cotangent).astype(BF))
    dy_all = over_y(dy)

    u = matmul(h2_all, wfc) + bfc
    g = gelu_tanh(u).astype(BF)
    dg = wide(dy_all, wproj)
    du = jax.vjp(gelu_tanh, u)[1](dg)[0].astype(BF)
    dh2 = summed_over_y(wide(du, wfc))

    result = (x2 + summed_over_y(matmul(g, wproj)) + bproj).astype(BF)
    output = matmul(deal, dealt(result)).astype(BF)

    dy_f = dy.astype(F32)
    dx2 = dy_f + norm_back(dh2, gain2, hat2, rate2)
    da = dx2.astype(BF)
    da_all = over_y(da)

    dattended = wide(da, wo).astype(BF).reshape(rows, heads, head)
    prob = jnp.exp(score_block() - log_total)
    dprob = jnp.einsum("rhd,kd->rhk", dattended, values, preferred_element_type=F32)
    inner = jnp.sum(prob * dprob, axis=2, keepdims=True)
    dscores = (prob * (dprob - inner)).astype(BF)
    dq = jnp.einsum("rhk,kd->rhd", dscores, keys, preferred_element_type=F32)
    dq = (dq * scale).reshape(rows, width).astype(BF)
    dkeys = jnp.einsum("rhk,rhd->kd", dscores, q_heads, preferred_element_type=F32) * scale
    dvalues = jnp.einsum("rhk,rhd->kd", prob.astype(BF), dattended, preferred_element_type=F32)
    dkv = jnp.concatenate([dkeys, dvalues], axis=1).astype(BF).reshape(nctx, rows, 2 * head)
    dkv = lax.all_to_all(dkv, CONTEXT, 0, 0, tiled=True)
    dkv = jnp.sum(dkv.astype(F32), axis=0).astype(BF)

    dq_theirs = swap(dq, XL)
    dh1_terms = wide(jnp.concatenate([dq, dq_theirs]), wq)
    dh1_mine = dh1_terms[:rows].reshape(rows, ny, shard)
    dh1_theirs = swap(dh1_terms[rows:].astype(BF), XL).astype(F32).reshape(rows, ny, shard)
    dh1 = jnp.moveaxis(pair(dh1_mine, dh1_theirs, xl), 0, 2).reshape(rows, width)
    dh1 = dh1 + wide(dkv, wkv)
    grad_hidden = (dx2 + norm_back(dh1, gain1, hat1, rate1)).astype(BF)

    def both_halves(array):
        theirs = swap(pick(array, co, 1).astype(BF), CORE)
        return pick(array, c, 1) + theirs.astype(F32)

    def both_x(array, dim):
        theirs = swap(pick(array, xo, dim).astype(BF), XL)
        return pick(array, xl, dim) + theirs.astype(F32)

    def spread(array):
        got = lax.all_to_all(array.astype(BF), ZX, 0, 0, tiled=True)
        return jnp.sum(got.astype(F32), axis=0).astype(BF)

    nzx = lax.axis_size(ZX)

    def collected(piece):
        mine = copies(piece, ZX)
        return pair(mine, swap(mine, CORE), c)

    dproj = tall(g, dy_all).reshape(2, 2, ff // 2, width)
    dfc = tall(h2_all, du).reshape(ny * 2, 2, half, block)
    dproj = both_x(both_halves(dproj), 0)
    dfc = both_x(both_halves(dfc).reshape(ny, 2, half, block), 1)
    part_proj = ff // 2 // nzx
    part_fc = half // nzx
    dproj = dproj.reshape(nzx, part_proj, width)
    dfc = jnp.moveaxis(dfc.reshape(ny, nzx, part_fc, block), 1, 0)
    both = jnp.concatenate([dproj, dfc.reshape(nzx, ny * part_fc, block)], axis=1)
    both = spread(both)
    dproj, dfc = both[:part_proj], both[part_proj:].reshape(ny, part_fc, block)
    got = [pick(dfc, y, 0)] + [shift(pick(dfc, (y + d) % ny, 0), Y, d) for d in range(1, ny)]
    got = jnp.stack(got)
    dfc = jnp.stack([pick(got, (y - k) % ny, 0) for k in range(ny)])
    both = collected(jnp.concatenate([dproj, dfc.reshape(ny * part_fc, block)]))
    grad_proj_w = both[:, :, :part_proj].reshape(ff, width).astype(F32)
    grad_fc_w = both[:, :, part_proj:].reshape(2, nzx, ny, part_fc, block)
    grad_fc_w = jnp.moveaxis(grad_fc_w, 2, 3).reshape(shard, ny * block).astype(F32)

    def columns(array):
        parts = array.reshape(rows, ny, 2 * shard)
        got = [pick(parts, y, 1)]
        got += [shift(pick(parts, (y + d) % ny, 1), Y, d) for d in range(1, ny)]
        return jnp.concatenate(got)

    def reduced(terms):
        terms = terms.reshape(2, 2, half, terms.shape[1])
        terms = both_x(both_halves(terms), 0)
        terms = spread(terms.reshape(nzx, part_fc, terms.shape[1]))
        return collected(terms).reshape(shard, terms.shape[1]).astype(F32)

    grad_out_w = reduced(tall(columns(attended), da_all))
    dqkv_all = over_y(jnp.concatenate([dq, dkv], axis=1))
    grad_qkv = reduced(tall(columns(h1), dqkv_all))

    def total(array):
        return jnp.sum(array.astype(F32), axis=0)

    vectors = [
        total(dy),
        total(dh2 * hat2),
        total(dh2),
        total(da),
        total(dq),
        total(dh1 * hat1),
        total(dh1),
    ]
    vectors = [v.reshape(2 * ny, shard) for v in vectors]
    du_sum = total(du).reshape(1, 2, ff)
    du_sum = lax.dynamic_update_slice(jnp.zeros((ny, 2, ff), F32), du_sum, (y, 0, 0))
    vectors += [du_sum.reshape(2 * ny, ff), total(dkv[:, head:]).reshape(2 * ny, -1)]
    sizes = [v.shape[1] for v in vectors]
    joined = jnp.concatenate(vectors, axis=1).astype(BF)
    joined = lax.all_to_all(joined, FSDP, 0, 0, tiled=True)
    joined = jnp.sum(joined.astype(F32), axis=0).astype(BF)
    joined = jnp.sum(copies(joined, CONTEXT).astype(F32), axis=0)
    ends = [sum(sizes[:k]) for k in range(1, len(sizes))]
    g_bproj, g_gain2, g_bias2, g_bo, g_bq, g_gain1, g_bias1, g_bfc, g_bv = jnp.split(joined, ends)

    maxima = jnp.max(copies(local_max, EVERY), axis=0)
    clip_ratio = CLIP_LIMIT / jnp.maximum(maxima, CLIP_LIMIT)
    column_scale = jnp.repeat(jnp.sqrt(clip_ratio), head)
    clipped_qw = query_weight.astype(F32) * column_scale[None, :]
    clipped_qb = query_bias.astype(F32) * lax.dynamic_slice_in_dim(
        column_scale, lax.axis_index(FSDP) * shard, shard
    )
    clipped_kw = kv_weight[:, :head].astype(F32) * jnp.sqrt(jnp.min(clip_ratio))
    return (
        output,
        grad_hidden,
        g_gain1,
        g_bias1,
        grad_qkv[:, :width],
        g_bq,
        grad_qkv[:, width:],
        g_bv,
        grad_out_w,
        g_bo,
        g_gain2,
        g_bias2,
        grad_fc_w,
        g_bfc,
        grad_proj_w,
        g_bproj,
        maxima,
        clipped_qw,
        clipped_qb,
        clipped_kw,
    )


def solution(mesh):
    torus = Mesh(mesh.devices.reshape(4, 2, 4, 2, 2), EVERY)
    tokens, table, vector, matrix = P(EVERY, None), P(FSDP, None), P(FSDP), P(FSDP, None)
    return jax.shard_map(
        shards,
        mesh=torus,
        in_specs=(
            tokens,
            tokens,
            table,
            table,
            table,
            vector,
            vector,
            matrix,
            vector,
            matrix,
            vector,
            matrix,
            vector,
            vector,
            vector,
            matrix,
            vector,
            matrix,
            vector,
        ),
        out_specs=(
            tokens,
            tokens,
            vector,
            vector,
            matrix,
            vector,
            matrix,
            vector,
            matrix,
            vector,
            vector,
            vector,
            matrix,
            vector,
            matrix,
            vector,
            P(),
            matrix,
            vector,
            matrix,
        ),
        check_vma=False,
    )
```

```python
import functools
import math

import jax
import jax.numpy as jnp
from jax import lax
from jax.experimental import pallas as pl
from jax.experimental.pallas import tpu as pltpu
from jax.sharding import Mesh
from jax.sharding import PartitionSpec as P

Y, XL, Z, XH, CORE = ("fsdp_0", "fsdp_1", "context_0", "context_1", "context_2")
FSDP = (Y, XL)
CONTEXT = (Z, XH, CORE)
ZX = (Z, XH)
EVERY = (Y, XL, Z, XH, CORE)

EPSILON = 1e-05
CLIP_LIMIT = 4.0
MASKED = -1e30
LANES = 128
BRIEF = pl.CostEstimate(flops=0, bytes_accessed=1024, transcendentals=0)
COST = pl.CostEstimate(flops=30_000_000_000, bytes_accessed=1024, transcendentals=0)
BF = jnp.bfloat16
F32 = jnp.float32


def shift(array, axis, by):
    n = lax.axis_size(axis)
    return lax.ppermute(array, axis, [(i, (i + by) % n) for i in range(n)])


def swap(array, axis):
    return shift(array, axis, 1)


def copies(array, axis):
    n = lax.axis_size(axis)
    return lax.all_to_all(jnp.broadcast_to(array[None], (n, *array.shape)), axis, 0, 0, tiled=True)


def gate(values, *done):
    return lax.optimization_barrier((values, done))[0]


def pick(array, index, dim):
    return lax.dynamic_index_in_dim(array, index, dim, keepdims=False)


def pair(own, other, index):
    return jnp.where(index == 0, jnp.stack([own, other]), jnp.stack([other, own]))


def numbers(values):
    return jnp.stack([jnp.asarray(v, jnp.int32) for v in values])


def cut(places, width, done=()):
    arrays = [array for array, _, _ in places]

    def kernel(at_ref, *refs):
        for source, out in zip(refs, refs[len(arrays) + len(done) :]):
            out[...] = source[...]

    def block_of(i):
        return lambda k, at: (at[2 * i], at[2 * i + 1])

    return pl.pallas_call(
        kernel,
        grid_spec=pltpu.PrefetchScalarGridSpec(
            num_scalar_prefetch=1,
            grid=(1,),
            in_specs=[pl.BlockSpec((LANES, width), block_of(i)) for i in range(len(arrays))]
            + [pl.BlockSpec(memory_space=pl.ANY)] * len(done),
            out_specs=[pl.BlockSpec((LANES, width), lambda k, at: (0, 0))] * len(arrays),
        ),
        out_shape=[jax.ShapeDtypeStruct((LANES, width), a.dtype) for a in arrays],
        compiler_params=pltpu.CompilerParams(vmem_limit_bytes=32 * 2**20),
        cost_estimate=COST,
        name="cut",
    )(numbers([n for _, row, column in places for n in (row, column)]), *arrays, *done)


def pack(shared, quarters, where):
    rows = [a.shape[0] for a in shared] + [2 * LANES] * len(quarters)
    wide = shared[0].shape[1]
    count = 8

    def kernel(at_ref, *refs):
        out, start = refs[-1], 0
        for k, length in enumerate(rows):
            if k < len(shared):
                out[0, start : start + length] = refs[k][...]
            else:
                out[0, start : start + LANES] = refs[k][:, :wide]
                out[0, start + LANES : start + length] = refs[k][:, wide:]
            start += length

    def block_of(i):
        return lambda k, at: (at[2 * (i * count + k)], at[2 * (i * count + k) + 1])

    return pl.pallas_call(
        kernel,
        grid_spec=pltpu.PrefetchScalarGridSpec(
            num_scalar_prefetch=1,
            grid=(count,),
            in_specs=[whole(*a.shape) for a in shared]
            + [pl.BlockSpec((LANES, 2 * wide), block_of(i)) for i in range(len(quarters))],
            out_specs=pl.BlockSpec((1, sum(rows), wide), lambda k, at: (k, 0, 0)),
        ),
        out_shape=jax.ShapeDtypeStruct((count, sum(rows), wide), BF),
        compiler_params=pltpu.CompilerParams(vmem_limit_bytes=32 * 2**20),
        cost_estimate=COST,
        name="pack",
    )(numbers([n for by in where for k in range(count) for n in by(k)]), *shared, *quarters)


def repeat_block(array, row, count, done=()):
    width = array.shape[1]

    def kernel(at_ref, in_ref, *refs):
        refs[-1][0] = in_ref[...]

    return pl.pallas_call(
        kernel,
        grid_spec=pltpu.PrefetchScalarGridSpec(
            num_scalar_prefetch=1,
            grid=(count,),
            in_specs=[pl.BlockSpec((LANES, width), lambda k, at: (at[0], 0))]
            + [pl.BlockSpec(memory_space=pl.ANY)] * len(done),
            out_specs=pl.BlockSpec((1, LANES, width), lambda k, at: (k, 0, 0)),
        ),
        out_shape=jax.ShapeDtypeStruct((count, LANES, width), BF),
        compiler_params=pltpu.CompilerParams(vmem_limit_bytes=32 * 2**20),
        cost_estimate=COST,
        name="repeat_block",
    )(numbers([row]), array, *done)


def assemble_quarters(pieces, core_and_z, cost, done=()):
    shards, _, wide = pieces[0].shape
    width = 8 * wide
    steps = 2 * len(pieces)

    def kernel(at_ref, *refs):
        for k, piece in enumerate(refs[: len(pieces)]):

            @pl.when(pl.program_id(0) // 2 == k)
            def _(piece=piece):
                refs[-1][...] = piece[...].reshape(shards, 1, LANES, wide)

    def block_of(i):
        return lambda k, at: (0, jnp.clip(k - 2 * i, 0, 1), 0)

    at = [n for core, z in core_and_z for j in (0, 1) for n in (core, 2 * z + j)]
    return pl.pallas_call(
        kernel,
        grid_spec=pltpu.PrefetchScalarGridSpec(
            num_scalar_prefetch=1,
            grid=(steps,),
            in_specs=[pl.BlockSpec((shards, LANES, wide), block_of(i)) for i in range(len(pieces))]
            + [pl.BlockSpec(memory_space=pl.ANY)] * len(done),
            out_specs=pl.BlockSpec(
                (shards, 1, LANES, wide), lambda k, at: (0, at[2 * k], 0, at[2 * k + 1])
            ),
        ),
        out_shape=jax.ShapeDtypeStruct((shards, 2, LANES, width), BF),
        compiler_params=pltpu.CompilerParams(vmem_limit_bytes=48 * 2**20),
        cost_estimate=cost,
        name="assemble_quarters",
    )(numbers(at), *pieces, *done).reshape(shards * 2 * LANES, width)


def side_by_side(full, parts, places):
    rows = parts[0].shape[0]
    part = 4 * LANES
    widths = [a.shape[1] for a in full] + [part] * len(parts)
    total, count, n = sum(widths), len(places), len(widths)

    def kernel(at_ref, *refs):
        for k, out in enumerate(refs[n:]):

            @pl.when(pl.program_id(0) == k)
            def _(out=out):
                start = 0
                for source, width in zip(refs[:n], widths):
                    out[:, start : start + width] = source[...]
                    start += width

    return pl.pallas_call(
        kernel,
        grid_spec=pltpu.PrefetchScalarGridSpec(
            num_scalar_prefetch=1,
            grid=(count,),
            in_specs=[whole(*a.shape) for a in full]
            + [pl.BlockSpec((rows, part), lambda k, at: (0, at[k]))] * len(parts),
            out_specs=[whole(rows, total)] * count,
        ),
        out_shape=[jax.ShapeDtypeStruct((rows, total), BF)] * count,
        compiler_params=pltpu.CompilerParams(vmem_limit_bytes=32 * 2**20),
        cost_estimate=COST,
        name="side_by_side",
    )(numbers(places), *full, *parts)


def assemble(pieces, rows, width, done=()):
    arrays = [a.reshape(-1, a.shape[-1]) for a, _, _ in pieces]
    counts = [a.shape[0] // LANES for a in arrays]
    firsts = [sum(counts[:k]) for k in range(len(counts))]
    steps = rows // LANES
    at = [o // LANES for _, _, offsets in pieces for o in offsets]

    def kernel(at_ref, *refs):
        step, out = pl.program_id(0), refs[-1]
        for source, first, count in zip(refs, firsts, counts):

            @pl.when((step >= first) & (step < first + count))
            def _(source=source):
                out[...] = source[...]

    def block_of(i):
        return lambda k, at: (jnp.clip(k - firsts[i], 0, counts[i] - 1), at[steps + i])

    return pl.pallas_call(
        kernel,
        grid_spec=pltpu.PrefetchScalarGridSpec(
            num_scalar_prefetch=1,
            grid=(steps,),
            in_specs=[pl.BlockSpec((LANES, width), block_of(i)) for i in range(len(arrays))]
            + [pl.BlockSpec(memory_space=pl.ANY)] * len(done),
            out_specs=pl.BlockSpec((LANES, width), lambda k, at: (at[k], 0)),
        ),
        out_shape=jax.ShapeDtypeStruct((rows, width), arrays[0].dtype),
        compiler_params=pltpu.CompilerParams(vmem_limit_bytes=32 * 2**20),
        cost_estimate=COST,
        name="assemble",
    )(numbers(at + [column for _, column, _ in pieces]), *arrays, *done)


def lay_both(pieces, at, proj_rows, fc_rows, count):
    steps = len(at)
    per = steps // 2
    columns = pieces[0].shape[-1]

    def kernel(at_ref, *refs):
        step = pl.program_id(0)
        proj_out, fc_out = refs[-2:]
        for k in range(steps):
            fc_ref = refs[(per + 1) * (k // per)]
            proj_ref = refs[(per + 1) * (k // per) + 1 + k % per]

            @pl.when(step == k)
            def _(fc_ref=fc_ref, proj_ref=proj_ref):
                part = proj_rows // 2
                for x in (0, 1):
                    for h in (0, 1):
                        proj_out[part * x : part * (x + 1), columns * h : columns * (h + 1)] = (
                            proj_ref[x, part * h : part * (h + 1)].astype(F32)
                        )
                    for j in range(count):
                        start = columns * (2 * j + x)
                        fc_out[:, start : start + columns] = fc_ref[
                            x, 0, fc_rows * j : fc_rows * (j + 1)
                        ].astype(F32)

    fc_rows_all = count * fc_rows

    def fc_block(i):
        return pl.BlockSpec(
            (2, 1, fc_rows_all, columns),
            lambda k, at: (0, jnp.clip(k - i * per, 0, per - 1), 0, 0),
        )

    specs = []
    for i in (0, 1):
        specs += [fc_block(i)] + [whole(*p.shape) for p in pieces[1 : per + 1]]
    shapes = [(proj_rows, 2 * columns), (fc_rows, 2 * count * columns)]
    return pl.pallas_call(
        kernel,
        grid_spec=pltpu.PrefetchScalarGridSpec(
            num_scalar_prefetch=1,
            grid=(steps,),
            in_specs=specs,
            out_specs=[pl.BlockSpec(shape, lambda k, at: (at[k], 0)) for shape in shapes],
        ),
        out_shape=[jax.ShapeDtypeStruct((steps * n, width), F32) for n, width in shapes],
        compiler_params=pltpu.CompilerParams(vmem_limit_bytes=56 * 2**20),
        cost_estimate=COST,
        name="lay_both",
    )(numbers(at), *pieces)


def add_cut(arrays, view, block, places):
    count, dims = len(places), len(view)

    def kernel(at_ref, *refs):
        total = functools.reduce(jnp.add, [r[...].astype(F32) for r in refs[: len(arrays)]])
        for k, out in enumerate(refs[len(arrays) :]):

            @pl.when(pl.program_id(0) == k)
            def _(out=out):
                out[...] = total.astype(BF)

    def index(k, at):
        return tuple(at[k * dims + i] for i in range(dims))

    return pl.pallas_call(
        kernel,
        grid_spec=pltpu.PrefetchScalarGridSpec(
            num_scalar_prefetch=1,
            grid=(count,),
            in_specs=[pl.BlockSpec(block, index)] * len(arrays),
            out_specs=[whole(*block)] * count,
        ),
        out_shape=[jax.ShapeDtypeStruct(block, BF)] * count,
        compiler_params=pltpu.CompilerParams(vmem_limit_bytes=40 * 2**20),
        cost_estimate=COST,
        name="add_cut",
    )(numbers([i for place in places for i in place]), *[a.reshape(view) for a in arrays])


def laid_out(mine, theirs, core, shapes, cut):
    count, rows, width = mine.shape

    def kernel(core_ref, mine_ref, theirs_ref, *outs):
        def write(piece):
            for out, value in zip(outs, cut(piece.astype(F32))):
                out[...] = value

        step = pl.program_id(0)

        @pl.when(step < count)
        def _():
            write(mine_ref[0])

        @pl.when(step >= count)
        def _():
            write(theirs_ref[0])

    def out_block(k, core_ref):
        own = (k < count).astype(jnp.int32)
        return (jnp.where(core_ref[0] == own, 1 - 0 * k, 0 * k) * count + k % count, 0)

    return pl.pallas_call(
        kernel,
        grid_spec=pltpu.PrefetchScalarGridSpec(
            num_scalar_prefetch=1,
            grid=(2 * count,),
            in_specs=[
                pl.BlockSpec((1, rows, width), lambda k, r: (jnp.minimum(k, count - 1), 0, 0)),
                pl.BlockSpec((1, rows, width), lambda k, r: (jnp.maximum(k - count, 0), 0, 0)),
            ],
            out_specs=[pl.BlockSpec(shape, out_block) for shape in shapes],
        ),
        out_shape=[
            jax.ShapeDtypeStruct((2 * count * n, columns), F32) for n, columns in shapes
        ],
        compiler_params=pltpu.CompilerParams(vmem_limit_bytes=32 * 2**20),
        cost_estimate=COST,
        name="laid_out",
    )(core.reshape(1).astype(jnp.int32), mine, theirs)


def matmul(left, right):
    return jnp.dot(left, right, preferred_element_type=F32)


def tall(left, right):
    return lax.dot_general(left, right, (((0,), (0,)), ((), ())), preferred_element_type=F32)


def wide(left, right):
    return lax.dot_general(left, right, (((1,), (1,)), ((), ())), preferred_element_type=F32)


def gelu_tanh(values):
    return jax.nn.gelu(values, approximate=True)


def whole(*shape):
    return pl.BlockSpec(shape, lambda *_: (0,) * len(shape))


def dot_wide(left, right):
    return lax.dot_general(left, right, (((1,), (1,)), ((), ())), preferred_element_type=F32)


def per_head(ref, first, count):
    return jnp.concatenate(
        [ref[first : first + count, k : k + LANES] for k in range(0, ref.shape[1], LANES)]
    )


def masked_scores(keys, queries, places, own, begin, step):
    scores = dot_wide(keys, queries)
    places = jnp.concatenate([places, places], axis=1)
    below = scores.shape[0] - step
    parts = []
    if below:
        parts.append(jnp.where(places[:below] >= begin, scores[:below], MASKED))
    near = (places[below:] >= begin) & (places[below:] <= own)
    parts.append(jnp.where(near, scores[below:], MASKED))
    return jnp.concatenate(parts) if below else parts[0]


def attend(q, kv, values_t, places, own, begin, scale, done=()):
    rows, width = q.shape
    groups = own.shape[0]
    part, step = rows // groups, kv.shape[0] // groups
    factor = scale * math.log2(math.e)

    def kernel(q_ref, kv_ref, vt_ref, place_ref, own_ref, begin_ref, *refs):
        out_ref, log_ref, top_ref = refs[len(done) :]
        for j in range(groups):
            n, row = step * (j + 1), slice(j, j + 1)
            scores = masked_scores(
                kv_ref[:n, :LANES],
                per_head(q_ref, part * j, part),
                place_ref[:n, :],
                own_ref[row, :],
                begin_ref[row, :],
                step,
            )
            top = jnp.max(scores, axis=0, keepdims=True)
            power = jnp.exp2((scores - top) * factor)
            total = jnp.sum(power, axis=0, keepdims=True)
            probs = (power * (1.0 / total)).astype(BF)
            out = jnp.dot(vt_ref[:, :n], probs, preferred_element_type=F32).T
            for k in range(width // LANES):
                out_ref[part * j : part * (j + 1), k * LANES : (k + 1) * LANES] = out[
                    part * k : part * (k + 1)
                ].astype(BF)
            log_ref[row, :] = top * factor + jnp.log2(total)
            top_ref[row, :] = top

    return pl.pallas_call(
        kernel,
        in_specs=[pl.BlockSpec(memory_space=pltpu.VMEM)] * 6
        + [pl.BlockSpec(memory_space=pl.ANY)] * len(done),
        out_shape=[
            jax.ShapeDtypeStruct((rows, width), BF),
            jax.ShapeDtypeStruct(own.shape, F32),
            jax.ShapeDtypeStruct(own.shape, F32),
        ],
        compiler_params=pltpu.CompilerParams(vmem_limit_bytes=48 * 2**20),
        cost_estimate=BRIEF,
        name="attend",
    )(q, kv, values_t, places, own, begin, *done)


def attend_back(q, grad, kv, keys_t, places, own, begin, logs, scale, done=()):
    rows, width = q.shape
    total = kv.shape[0]
    groups = own.shape[0]
    part, step = rows // groups, total // groups
    factor = scale * math.log2(math.e)

    def kernel(
        q_ref, g_ref, kv_ref, kt_ref, place_ref, own_ref, begin_ref, log_ref, *refs
    ):
        dq_ref, dkv_ref, acc_ref = refs[len(done) :]
        for j in reversed(range(groups)):
            n, row = step * (j + 1), slice(j, j + 1)
            queries = per_head(q_ref, part * j, part)
            grads = per_head(g_ref, part * j, part)
            scores = masked_scores(
                kv_ref[:n, :LANES],
                queries,
                place_ref[:n, :],
                own_ref[row, :],
                begin_ref[row, :],
                step,
            )
            prob = jnp.exp2(scores * factor - log_ref[row, :])
            dprob = dot_wide(kv_ref[:n, LANES:], grads)
            inner = jnp.sum(prob * dprob, axis=0, keepdims=True)
            dscores = (prob * (dprob - inner)).astype(BF)
            dq = jnp.dot(kt_ref[:, :n], dscores, preferred_element_type=F32).T * scale
            for k in range(width // LANES):
                dq_ref[part * j : part * (j + 1), k * LANES : (k + 1) * LANES] = dq[
                    part * k : part * (k + 1)
                ].astype(BF)
            dkeys = jnp.dot(dscores, queries, preferred_element_type=F32)
            dvalues = jnp.dot(prob.astype(BF), grads, preferred_element_type=F32)
            if j == groups - 1:
                acc_ref[:, :LANES] = dkeys
                acc_ref[:, LANES:] = dvalues
            else:
                acc_ref[:n, :LANES] += dkeys
                acc_ref[:n, LANES:] += dvalues
        dkv_ref[:, :LANES] = (acc_ref[:, :LANES] * scale).astype(BF)
        dkv_ref[:, LANES:] = acc_ref[:, LANES:].astype(BF)

    return pl.pallas_call(
        kernel,
        in_specs=[pl.BlockSpec(memory_space=pltpu.VMEM)] * 8
        + [pl.BlockSpec(memory_space=pl.ANY)] * len(done),
        out_shape=[
            jax.ShapeDtypeStruct((rows, width), BF),
            jax.ShapeDtypeStruct(kv.shape, BF),
        ],
        scratch_shapes=[pltpu.VMEM(kv.shape, F32)],
        compiler_params=pltpu.CompilerParams(vmem_limit_bytes=48 * 2**20),
        cost_estimate=COST,
        name="attend_back",
    )(q, grad, kv, keys_t, places, own, begin, logs, *done)


def feed_forward(h, dy, w_fc, b_fc, w_proj, done=()):
    tokens, width = h.shape
    units, part = w_fc.shape[1], 512
    curve = math.sqrt(2.0 / math.pi)

    def kernel(h_ref, dy_ref, fc_ref, b_ref, proj_ref, *refs):
        g_ref, du_ref, sum_ref, dh_ref, acc_ref = refs[len(done) :]
        step = pl.program_id(0)
        u = jnp.dot(h_ref[...], fc_ref[...], preferred_element_type=F32) + b_ref[...]
        dg = dot_wide(dy_ref[...], proj_ref[...])
        square = u * u
        bend = jnp.tanh(curve * u * (1.0 + 0.044715 * square))
        half = 0.5 + 0.5 * bend
        g_ref[...] = (u * half).astype(BF)
        slope = half + 0.5 * curve * u * (1.0 - bend * bend) * (1.0 + 3 * 0.044715 * square)
        du = (dg * slope).astype(BF)
        du_ref[...] = du
        sum_ref[...] = jnp.sum(du.astype(F32), axis=0, keepdims=True)
        term = dot_wide(du, fc_ref[...])

        @pl.when(step == 0)
        def _():
            acc_ref[...] = term

        @pl.when(step > 0)
        def _():
            acc_ref[...] += term

        @pl.when(step == units // part - 1)
        def _():
            dh_ref[...] = acc_ref[...].astype(BF)

    along = lambda k: (0, k)
    return pl.pallas_call(
        kernel,
        grid=(units // part,),
        in_specs=[
            whole(tokens, width),
            whole(tokens, width),
            pl.BlockSpec((width, part), along),
            pl.BlockSpec((1, part), along),
            pl.BlockSpec((part, width), lambda k: (k, 0)),
        ]
        + [pl.BlockSpec(memory_space=pl.ANY)] * len(done),
        out_specs=[
            pl.BlockSpec((tokens, part), along),
            pl.BlockSpec((tokens, part), along),
            pl.BlockSpec((1, part), along),
            whole(tokens, width),
        ],
        out_shape=[
            jax.ShapeDtypeStruct((tokens, units), BF),
            jax.ShapeDtypeStruct((tokens, units), BF),
            jax.ShapeDtypeStruct((1, units), F32),
            jax.ShapeDtypeStruct((tokens, width), BF),
        ],
        scratch_shapes=[pltpu.VMEM((tokens, width), F32)],
        compiler_params=pltpu.CompilerParams(vmem_limit_bytes=56 * 2**20),
        cost_estimate=COST,
        name="feed_forward",
    )(h, dy, w_fc, b_fc.reshape(1, units), w_proj, *done)


def products(pairs, at_left, at_right, extra=None, split=False):
    outs, per = len(at_left), len(at_left[0])
    tokens = pairs[0][0].shape[0]
    widths = [w for _, _, w in pairs]
    n, total = len(pairs), sum(widths)
    rows = per * LANES

    def kernel(at_ref, *refs):
        values, start = [], 0
        for i, width in enumerate(widths):
            own = refs[i * (per + 1) : (i + 1) * (per + 1)]
            left = jnp.concatenate([r[...] for r in own[:per]], axis=1)
            value = lax.dot_general(
                left, own[per][...], (((0,), (0,)), ((), ())), preferred_element_type=F32
            )
            if extra is not None:
                value = value + refs[n * (per + 1)][:, start : start + width].astype(F32)
            values.append(value.astype(BF))
            start += width

        def write(out):
            start = 0
            for value, width in zip(values, widths):
                out[:, start : start + width] = value
                start += width

        for k, out in enumerate(refs[n * (per + 1) + (extra is not None) :]):
            if split:
                pl.when(pl.program_id(0) == k)(functools.partial(write, out))
            else:
                write(out)

    def left_block(j):
        return lambda k, at: (0, at[k * per + j])

    def right_block(k, at):
        return (0, at[outs * per + k])

    specs, operands = [], []
    for left, right, width in pairs:
        specs += [pl.BlockSpec((tokens, LANES), left_block(j)) for j in range(per)]
        specs.append(pl.BlockSpec((tokens, width), right_block))
        operands += [left] * per + [right]
    if extra is not None:
        specs.append(pl.BlockSpec((rows, total), lambda k, at: (k, 0)))
        operands.append(extra)
    if split:
        out_specs = [whole(rows, total)] * outs
        out_shape = [jax.ShapeDtypeStruct((rows, total), BF)] * outs
    else:
        out_specs = [pl.BlockSpec((rows, total), lambda k, at: (k, 0))]
        out_shape = [jax.ShapeDtypeStruct((outs * rows, total), BF)]
    return pl.pallas_call(
        kernel,
        grid_spec=pltpu.PrefetchScalarGridSpec(
            num_scalar_prefetch=1, grid=(outs,), in_specs=specs, out_specs=out_specs
        ),
        out_shape=out_shape,
        compiler_params=pltpu.CompilerParams(vmem_limit_bytes=56 * 2**20),
        cost_estimate=COST,
        name="products",
    )(numbers([i for row in at_left for i in row] + list(at_right)), *operands)


def norm_parts(values):
    centered = values - jnp.mean(values, axis=-1, keepdims=True)
    rate = lax.rsqrt(jnp.mean(centered * centered, axis=-1, keepdims=True) + EPSILON)
    return centered * rate, rate


def norm_back(grad, gain, hat, rate):
    e = grad * gain
    inner = jnp.mean(e * hat, axis=-1, keepdims=True)
    return rate * (e - jnp.mean(e, axis=-1, keepdims=True) - hat * inner)


def shards(
    hidden,
    cotangent,
    lengths,
    source_pos,
    owner_slot,
    ln1_gain,
    ln1_bias,
    query_weight,
    query_bias,
    kv_weight,
    value_bias,
    out_weight,
    out_bias,
    ln2_gain,
    ln2_bias,
    fc_weight,
    fc_bias,
    proj_weight,
    proj_bias,
):
    rows, width = hidden.shape
    ny, nz, nctx = lax.axis_size(Y), lax.axis_size(Z), lax.axis_size(CONTEXT)
    y, xl, z, c = (lax.axis_index(a) for a in (Y, XL, Z, CORE))
    xo, co = 1 - xl, 1 - c
    ctx = lax.axis_index(CONTEXT)
    sub = rows // nctx
    head = kv_weight.shape[1] // 2
    heads = width // head
    scale = 1.0 / math.sqrt(head)
    shard = query_weight.shape[0]
    nzx = lax.axis_size(ZX)
    half = shard // 2
    ff = proj_weight.shape[0]
    block = 2 * ff

    small = jnp.concatenate(
        [
            jnp.stack([ln1_gain, ln1_bias, query_bias, out_bias, ln2_gain, ln2_bias, proj_bias]),
            jnp.pad(value_bias, (0, shard - value_bias.shape[0]))[None],
            fc_bias.reshape(-1, shard),
            jnp.zeros((4, shard), BF),
        ]
    )
    first = pack(
        [small, kv_weight],
        [out_weight, fc_weight],
        [lambda k: (c, z), lambda k: (c, k // 2 * nz + z)],
    )
    first = lax.all_to_all(first, FSDP, 0, 0, tiled=True)
    small = first[:, :16]
    gain1, bias1, bq, bo, gain2, bias2, bproj = (
        small[:, k].reshape(width).astype(F32) for k in range(7)
    )
    bv = small[:, 7, : value_bias.shape[0]].reshape(head).astype(F32)
    bfc = pick(small[:, 8:12].reshape(ny, block), y, 0).astype(F32)
    wkv = first[:, 16 : 16 + shard].reshape(width, 2 * head)

    q_mine = lax.all_to_all(
        repeat_block(query_weight, c, 2 * ny, (first,)), FSDP, 0, 0, tiled=True
    )

    def quarters(piece):
        return [piece] + [shift(piece, Z, d) for d in range(1, nz)]

    def whole_weight(mine, theirs, cost):
        there = [(z - d) % nz for d in range(nz)]
        return assemble_quarters(
            mine + theirs, [(c, k) for k in there] + [(co, k) for k in there], cost
        )

    at = 16 + shard
    o_mine = quarters(first[:, at : at + shard])

    x = hidden.astype(F32)
    hat1, rate1 = norm_parts(x)
    h1 = (hat1 * gain1 + bias1).astype(BF)
    kv = matmul(h1, wkv) + jnp.concatenate([jnp.zeros((head,), F32), bv])
    owned = lax.dynamic_slice_in_dim(owner_slot[0], ctx * rows, rows)
    target = owned // rows * sub + owned % rows - ctx * sub
    deal = (target[:, None] == jnp.arange(rows, dtype=jnp.int32)[None, :]).astype(BF)

    def dealt(array):
        pieces = array.astype(BF).reshape(nctx, sub, width)
        return lax.all_to_all(pieces, CONTEXT, 0, 0, tiled=True).reshape(rows, width)

    dealing = tall(deal, cotangent).astype(BF).reshape(nctx, -1, 2 * head)
    kv, q_mine, o_mine, dealing = gate((kv.astype(BF), q_mine, o_mine, dealing))
    q_theirs, o_theirs = swap(q_mine, CORE), [swap(m, CORE) for m in o_mine]
    kv = jnp.broadcast_to(kv[None], (nctx, rows, 2 * head))
    all_kv = lax.all_to_all(jnp.concatenate([kv, dealing], axis=1), CONTEXT, 0, 0, tiled=True)
    shards_at = [shard * k for k in range(2 * ny)]
    wq = assemble(
        [
            (q_mine, 0, [a + half * c for a in shards_at]),
            (q_theirs, 0, [a + half * co for a in shards_at]),
        ],
        width,
        width,
    )
    all_kv, wq, o_mine, o_theirs, proj_weight, first = gate(
        (all_kv, wq, o_mine, o_theirs, proj_weight, first)
    )
    dy = all_kv[:, rows:].reshape(rows, width)
    all_kv = all_kv[:, :rows]
    f_mine = quarters(first[:, at + shard :])
    p_mine = swap(lax.dynamic_slice_in_dim(proj_weight, ff // 2 * c, ff // 2), XL)
    wo = whole_weight(o_mine, o_theirs, BRIEF)
    q = (matmul(h1, wq) + bq).astype(BF)

    positions = source_pos[0]
    starts = jnp.cumsum(lengths[0]) - lengths[0]
    own_pos = lax.dynamic_slice_in_dim(positions, ctx * rows, rows)
    seq_start = jnp.max(jnp.where(starts[None, :] <= own_pos[:, None], starts[None, :], 0), axis=1)
    groups = rows // 16
    natural = jnp.moveaxis(all_kv.reshape(nctx, nctx, sub, 2 * head), 0, 1)
    natural = natural.reshape(nctx * rows, 2 * head)
    xh = lax.axis_index(XH)
    places = jnp.moveaxis(positions.reshape(nctx, nctx, sub), 0, 1).reshape(nctx * rows, 1)
    places = jnp.broadcast_to(places, (nctx * rows, LANES))

    def for_heads(array):
        array = jnp.broadcast_to(array.reshape(groups, 1, 16), (groups, heads, 16))
        return array.reshape(groups, heads * 16)

    own, begin = for_heads(own_pos), for_heads(seq_start)
    attended, logs, tops = attend(
        q, natural, natural[:, head:].T, places, own, begin, scale
    )
    local_max = jnp.max(tops.reshape(groups, heads, 16), axis=(0, 2)) * scale

    def pieces_of(array):
        return [array] + [shift(array, Y, d) for d in range(1, ny)]

    dy_pieces = pieces_of(dy)
    attended, wo, f_mine, dy_pieces, p_mine = gate((attended, wo, f_mine, dy_pieces, p_mine))
    x2 = x + matmul(attended, wo) + bo
    hat2, rate2 = norm_parts(x2)
    h2 = (hat2 * gain2 + bias2).astype(BF)

    def over_y(array):
        return jnp.concatenate(pieces_of(array))

    h2, f_mine, p_mine = gate((h2, f_mine, p_mine))
    dy_all = jnp.concatenate(dy_pieces)
    h2_pieces = pieces_of(h2)
    wfc = whole_weight(f_mine, [swap(m, CORE) for m in f_mine], COST)
    p_theirs = swap(p_mine, CORE)
    wproj = assemble(
        [
            (proj_weight, 0, [ff * xl + LANES * k for k in range(ff // LANES)]),
            (p_mine, 0, [ff * xo + ff // 2 * c + LANES * k for k in range(ff // 2 // LANES)]),
            (p_theirs, 0, [ff * xo + ff // 2 * co + LANES * k for k in range(ff // 2 // LANES)]),
        ],
        block,
        width,
    )
    h2_pieces, wfc, wproj = gate((h2_pieces, wfc, wproj))
    h2_all = jnp.concatenate(h2_pieces)
    g, du, du_sum, dh2 = feed_forward(h2_all, dy_all, wfc, bfc, wproj)

    x_ring = [(a, b) for a in (0, 1) for b in (0, 1)]
    zs = [(z + d) % nz for d in range(nz)]
    part_z = half // nz

    def flip(array, a, b):
        moves = [(2 * i + j, 2 * (i ^ a) + (j ^ b)) for i in (0, 1) for j in (0, 1)]
        return lax.ppermute(array, (XL, XH), moves)

    def over_x(parts):
        return [parts[0]] + [flip(p, a, b) for p, (a, b) in zip(parts[1:], x_ring[1:])]

    def over_z(parts):
        return [parts[0]] + [shift(parts[d], Z, d) for d in range(1, nz)]

    def core_summed(pairs, left_at, right_at):
        (theirs,) = products(pairs, left_at(co), right_at)
        return products(pairs, left_at(c), right_at, swap(theirs, CORE), True)

    dproj = core_summed(
        [(g, dy_all, width)],
        lambda core: [[(k * 2 + core) * nz + there for k in (0, 1)] for there in zs],
        [0] * nz,
    )
    dh2 = dh2.reshape(ny, rows, width)
    dh2 = [dh2[0]] + [shift(dh2[d], Y, -d) for d in range(1, ny)]
    dh2, dproj, attended, h1 = gate((dh2, dproj, attended, h1))
    dproj = over_z(dproj)
    sent = side_by_side([], [attended, h1], [(y + d) % ny for d in range(ny)])
    sent = [sent[0]] + [shift(sent[d], Y, d) for d in range(1, ny)]
    dh2 = functools.reduce(jnp.add, [t.astype(F32) for t in dh2])

    dy_f = dy.astype(F32)
    dx2 = dy_f + norm_back(dh2, gain2, hat2, rate2)
    da = dx2.astype(BF)

    dattended = wide(da, wo).astype(BF)
    dq, dkv = attend_back(
        q, dattended, natural, natural[:, :head].T, places, own, begin, logs, scale
    )
    dfc = core_summed(
        [(h2_all, du, block // 2)],
        lambda core: [[(k * 2 + (xl ^ a)) * 2 + core for k in range(ny)] for a, _ in x_ring],
        [xh ^ b for _, b in x_ring],
    )
    dq, dkv, da, dproj, dfc, g, sent = gate((dq, dkv, da, dproj, dfc, g, sent))
    dfc = over_x(dfc)
    sent = jnp.concatenate(sent)
    attended_columns, h1_columns = sent[:, : block // ny], sent[:, block // ny :]
    dkv = jnp.moveaxis(dkv.reshape(nctx, nz, 2, 2, sub, 2 * head), 0, 3)
    dkv = dkv.reshape(nz, 2, 2, rows, 2 * head)

    def plus(mine, *got):
        return functools.reduce(jnp.add, [t.astype(F32) for t in (mine, *got)]).astype(BF)

    dkv = plus(pick(dkv, c, 2), swap(pick(dkv, co, 2), CORE))
    dkv = plus(pick(dkv, xh, 1), swap(pick(dkv, 1 - xh, 1), XH))
    dkv = plus(pick(dkv, z, 0), *[shift(pick(dkv, k, 0), Z, d) for d, k in list(enumerate(zs))[1:]])
    da_dq = over_y(jnp.concatenate([da, dq], axis=1))
    result_terms = matmul(g, wproj).astype(BF)

    dproj, dfc, da_dq, dkv, result_terms, dq = gate(
        (dproj, dfc, da_dq, dkv, result_terms, dq)
    )
    dh1 = wide(dq, wq)
    dproj = add_cut(
        dproj,
        (2, 2, half // 2, width),
        (1, 1, half // 2, width),
        [(xl ^ a, xh ^ b, 0, 0) for a, b in x_ring],
    )
    dproj = over_x(dproj)
    dfc = add_cut(
        dfc,
        (ny, nz, part_z, block // 2),
        (ny, 1, part_z, block // 2),
        [(0, there, 0, 0) for there in zs],
    )
    dfc = over_z(dfc)
    dkv_all = over_y(dkv)
    part_fc = half // nzx

    def spread(terms):
        terms = terms.reshape(2 * nzx, part_fc, -1)
        return lax.all_to_all(terms, (XL,) + ZX, 0, 0, tiled=True)

    da_all, dq_all = da_dq[:, :width], da_dq[:, width:]
    (theirs,) = products([(attended_columns, da_all, width)], [[co, 2 + co]], [0])
    (dwo,) = products(
        [(attended_columns, da_all, width)], [[c, 2 + c]], [0], swap(theirs, CORE)
    )
    dwo = spread(dwo)
    result = result_terms.reshape(ny, rows, width)
    result = [result[0]] + [shift(result[d], Y, -d) for d in range(1, ny)]
    dproj, dfc, dkv_all, result, dh1, dwo = gate((dproj, dfc, dkv_all, result, dh1, dwo))
    dproj = add_cut(
        dproj,
        (half // 2, width),
        (half // 2, width // 2),
        [(0, 0), (0, 1)],
    )
    dproj = jnp.concatenate(dproj)
    dproj_other = swap(dproj, XH)
    dfc = add_cut(
        dfc,
        (ny, part_z, block // 2),
        (1, part_z, block // 2),
        [((y + d) % ny, 0, 0) for d in range(ny)],
    )
    dfc = [dfc[0]] + [shift(dfc[d], Y, d) for d in range(1, ny)]
    dfc, dproj, dproj_other = gate((dfc, dproj, dproj_other))
    dfc = jnp.stack(dfc)

    dfc = jnp.concatenate([pick(dfc, (y - k) % ny, 0)[0] for k in range(ny)])
    there = [(z - d) % nz for d in range(nz)]
    dfc = [dfc] + [shift(dfc, Z, d) for d in range(1, nz)]
    pairs = [(h1_columns, dq_all, width), (h1_columns, dkv_all, 2 * head)]
    (theirs,) = products(pairs, [[co, 2 + co]], [0])
    (dwq,) = products(pairs, [[c, 2 + c]], [0], swap(theirs, CORE))
    dh1 = dh1 + wide(dkv, wkv)
    grad_hidden = (dx2 + norm_back(dh1, gain1, hat1, rate1)).astype(BF)
    result = functools.reduce(jnp.add, [t.astype(F32) for t in result])
    result = dealt((x2 + result + bproj).astype(BF))
    def total(array):
        return jnp.sum(array.astype(F32), axis=0)

    vectors = [
        total(dy),
        total(dh2 * hat2),
        total(dh2),
        total(da),
        total(dq),
        total(dh1 * hat1),
        total(dh1),
    ]
    vectors = [v.reshape(2 * ny, 1, shard) for v in vectors]
    du_sum = du_sum.reshape(1, 2, ff // shard, shard)
    du_sum = lax.dynamic_update_slice(
        jnp.zeros((ny, 2, ff // shard, shard), F32), du_sum, (y, 0, 0, 0)
    )
    bv_sum = total(dkv[:, head:]).reshape(2 * ny, 1, -1)
    top_high = lax.reduce_precision(local_max, 8, 7)
    tops = jnp.concatenate([top_high, local_max - top_high])
    tops = jnp.broadcast_to(tops, (2 * ny, 1, 2 * heads))
    last = [jnp.pad(v, ((0, 0), (0, 0), (0, shard - v.shape[2]))) for v in (bv_sum, tops)]
    vectors += [du_sum.reshape(2 * ny, -1, shard), *last]
    joined = jnp.concatenate(vectors, axis=1).astype(BF)
    joined = jnp.pad(joined, ((0, 0), (0, 16 - joined.shape[1]), (0, 0)))
    joined = jnp.broadcast_to(joined[:, None], (2 * ny, nctx, *joined.shape[1:]))
    joined = joined.reshape(-1, 16, shard)
    joined = lax.all_to_all(joined, EVERY, 0, 0, tiled=True)
    dfc, dwq, dwo, dproj, dproj_other, result, joined = gate(
        (dfc, dwq, dwo, dproj, dproj_other, result, joined)
    )
    output = matmul(deal, result).astype(BF)

    dfc = jnp.stack(dfc)
    dfc_other = swap(dfc, XH)
    dproj = pair(dproj, dproj_other, xh)
    dproj = [dproj] + [shift(dproj, Z, d) for d in range(1, nz)]
    small_w = jnp.concatenate([dwo, spread(dwq)], axis=2)
    dfc, dfc_other, dproj, small_w = gate((dfc, dfc_other, dproj, small_w))
    small_w = copies(jnp.sum(small_w.astype(F32), axis=0).astype(BF), ZX)
    dfc = pair(dfc, dfc_other, xh)
    mine = [dfc] + dproj
    mine = mine + [swap(m, CORE) for m in mine]
    grad_proj_w, grad_fc_w = lay_both(
        mine,
        [c * nz + k for k in there] + [co * nz + k for k in there],
        half,
        part_z,
        ny,
    )
    small_w, grad_proj_w, grad_fc_w = gate((small_w, grad_proj_w, grad_fc_w))
    grad_out_w, grad_query_w, grad_kv_w = laid_out(
        small_w,
        swap(small_w, CORE),
        c,
        [(part_fc, width), (part_fc, width), (part_fc, 2 * head)],
        lambda piece: (piece[:, :width], piece[:, width : 2 * width], piece[:, 2 * width :]),
    )

    tops = joined[:, 12].astype(F32)
    maxima = jnp.max(tops[:, :heads] + tops[:, heads : 2 * heads], axis=0)
    joined = jnp.sum(joined.astype(F32), axis=0)
    g_bproj, g_gain2, g_bias2, g_bo, g_bq, g_gain1, g_bias1 = (joined[k] for k in range(7))
    g_bfc, g_bv = joined[7:11].reshape(ff), joined[11, : value_bias.shape[0]]

    clip_ratio = CLIP_LIMIT / jnp.maximum(maxima, CLIP_LIMIT)
    column_scale = jnp.repeat(jnp.sqrt(clip_ratio), head)
    clipped_qw = query_weight.astype(F32) * column_scale[None, :]
    clipped_qb = query_bias.astype(F32) * lax.dynamic_slice_in_dim(
        column_scale, lax.axis_index(FSDP) * shard, shard
    )
    clipped_kw = kv_weight[:, :head].astype(F32) * jnp.sqrt(jnp.min(clip_ratio))
    return (
        output,
        grad_hidden,
        g_gain1,
        g_bias1,
        grad_query_w,
        g_bq,
        grad_kv_w,
        g_bv,
        grad_out_w,
        g_bo,
        g_gain2,
        g_bias2,
        grad_fc_w,
        g_bfc,
        grad_proj_w,
        g_bproj,
        maxima,
        clipped_qw,
        clipped_qb,
        clipped_kw,
    )


def solution(mesh):
    torus = Mesh(mesh.devices.reshape(4, 2, 4, 2, 2), EVERY)
    tokens, table, vector, matrix = P(EVERY, None), P(FSDP, None), P(FSDP), P(FSDP, None)
    return jax.shard_map(
        shards,
        mesh=torus,
        in_specs=(
            tokens,
            tokens,
            table,
            table,
            table,
            vector,
            vector,
            matrix,
            vector,
            matrix,
            vector,
            matrix,
            vector,
            vector,
            vector,
            matrix,
            vector,
            matrix,
            vector,
        ),
        out_specs=(
            tokens,
            tokens,
            vector,
            vector,
            matrix,
            vector,
            matrix,
            vector,
            matrix,
            vector,
            vector,
            vector,
            matrix,
            vector,
            matrix,
            vector,
            P(),
            matrix,
            vector,
            matrix,
        ),
        check_vma=False,
    )
```

```python
import functools
import math

import jax
import jax.numpy as jnp
from jax import lax
from jax.experimental import pallas as pl
from jax.experimental.pallas import tpu as pltpu
from jax.sharding import Mesh
from jax.sharding import PartitionSpec as P

Y, XL, Z, XH, CORE = ("fsdp_0", "fsdp_1", "context_0", "context_1", "context_2")
FSDP = (Y, XL)
CONTEXT = (Z, XH, CORE)
ZX = (Z, XH)
EVERY = (Y, XL, Z, XH, CORE)

EPSILON = 1e-05
CLIP_LIMIT = 4.0
MASKED = -1e30
LANES = 128
BRIEF = pl.CostEstimate(flops=0, bytes_accessed=1024, transcendentals=0)
COST = pl.CostEstimate(flops=30_000_000_000, bytes_accessed=1024, transcendentals=0)
BF = jnp.bfloat16
F32 = jnp.float32


def shift(array, axis, by):
    n = lax.axis_size(axis)
    return lax.ppermute(array, axis, [(i, (i + by) % n) for i in range(n)])


def swap(array, axis):
    return shift(array, axis, 1)


def copies(array, axis):
    n = lax.axis_size(axis)
    return lax.all_to_all(jnp.broadcast_to(array[None], (n, *array.shape)), axis, 0, 0, tiled=True)


def gate(values, *done):
    return lax.optimization_barrier((values, done))[0]


def pick(array, index, dim):
    return lax.dynamic_index_in_dim(array, index, dim, keepdims=False)


def pair(own, other, index):
    return jnp.where(index == 0, jnp.stack([own, other]), jnp.stack([other, own]))


def numbers(values):
    return jnp.stack([jnp.asarray(v, jnp.int32) for v in values])


def cut(places, width, done=()):
    arrays = [array for array, _, _ in places]

    def kernel(at_ref, *refs):
        for source, out in zip(refs, refs[len(arrays) + len(done) :]):
            out[...] = source[...]

    def block_of(i):
        return lambda k, at: (at[2 * i], at[2 * i + 1])

    return pl.pallas_call(
        kernel,
        grid_spec=pltpu.PrefetchScalarGridSpec(
            num_scalar_prefetch=1,
            grid=(1,),
            in_specs=[pl.BlockSpec((LANES, width), block_of(i)) for i in range(len(arrays))]
            + [pl.BlockSpec(memory_space=pl.ANY)] * len(done),
            out_specs=[pl.BlockSpec((LANES, width), lambda k, at: (0, 0))] * len(arrays),
        ),
        out_shape=[jax.ShapeDtypeStruct((LANES, width), a.dtype) for a in arrays],
        compiler_params=pltpu.CompilerParams(vmem_limit_bytes=32 * 2**20),
        cost_estimate=COST,
        name="cut",
    )(numbers([n for _, row, column in places for n in (row, column)]), *arrays, *done)


def pack(shared, quarters, where):
    rows = [a.shape[0] for a in shared] + [2 * LANES] * len(quarters)
    wide = shared[0].shape[1]
    count = 8

    def kernel(at_ref, *refs):
        out, start = refs[-1], 0
        for k, length in enumerate(rows):
            if k < len(shared):
                out[0, start : start + length] = refs[k][...]
            else:
                out[0, start : start + LANES] = refs[k][:, :wide]
                out[0, start + LANES : start + length] = refs[k][:, wide:]
            start += length

    def block_of(i):
        return lambda k, at: (at[2 * (i * count + k)], at[2 * (i * count + k) + 1])

    return pl.pallas_call(
        kernel,
        grid_spec=pltpu.PrefetchScalarGridSpec(
            num_scalar_prefetch=1,
            grid=(count,),
            in_specs=[whole(*a.shape) for a in shared]
            + [pl.BlockSpec((LANES, 2 * wide), block_of(i)) for i in range(len(quarters))],
            out_specs=pl.BlockSpec((1, sum(rows), wide), lambda k, at: (k, 0, 0)),
        ),
        out_shape=jax.ShapeDtypeStruct((count, sum(rows), wide), BF),
        compiler_params=pltpu.CompilerParams(vmem_limit_bytes=32 * 2**20),
        cost_estimate=COST,
        name="pack",
    )(numbers([n for by in where for k in range(count) for n in by(k)]), *shared, *quarters)


def repeat_block(array, row, count, done=()):
    width = array.shape[1]

    def kernel(at_ref, in_ref, *refs):
        refs[-1][0] = in_ref[...]

    return pl.pallas_call(
        kernel,
        grid_spec=pltpu.PrefetchScalarGridSpec(
            num_scalar_prefetch=1,
            grid=(count,),
            in_specs=[pl.BlockSpec((LANES, width), lambda k, at: (at[0], 0))]
            + [pl.BlockSpec(memory_space=pl.ANY)] * len(done),
            out_specs=pl.BlockSpec((1, LANES, width), lambda k, at: (k, 0, 0)),
        ),
        out_shape=jax.ShapeDtypeStruct((count, LANES, width), BF),
        compiler_params=pltpu.CompilerParams(vmem_limit_bytes=32 * 2**20),
        cost_estimate=COST,
        name="repeat_block",
    )(numbers([row]), array, *done)


def assemble_quarters(pieces, core_and_z, cost, done=()):
    shards, _, wide = pieces[0].shape
    width = 8 * wide
    steps = 2 * len(pieces)

    def kernel(at_ref, *refs):
        for k, piece in enumerate(refs[: len(pieces)]):

            @pl.when(pl.program_id(0) // 2 == k)
            def _(piece=piece):
                refs[-1][...] = piece[...].reshape(shards, 1, LANES, wide)

    def block_of(i):
        return lambda k, at: (0, jnp.clip(k - 2 * i, 0, 1), 0)

    at = [n for core, z in core_and_z for j in (0, 1) for n in (core, 2 * z + j)]
    return pl.pallas_call(
        kernel,
        grid_spec=pltpu.PrefetchScalarGridSpec(
            num_scalar_prefetch=1,
            grid=(steps,),
            in_specs=[pl.BlockSpec((shards, LANES, wide), block_of(i)) for i in range(len(pieces))]
            + [pl.BlockSpec(memory_space=pl.ANY)] * len(done),
            out_specs=pl.BlockSpec(
                (shards, 1, LANES, wide), lambda k, at: (0, at[2 * k], 0, at[2 * k + 1])
            ),
        ),
        out_shape=jax.ShapeDtypeStruct((shards, 2, LANES, width), BF),
        compiler_params=pltpu.CompilerParams(vmem_limit_bytes=48 * 2**20),
        cost_estimate=cost,
        name="assemble_quarters",
    )(numbers(at), *pieces, *done).reshape(shards * 2 * LANES, width)


def side_by_side(full, parts, places):
    rows = parts[0].shape[0]
    part = 4 * LANES
    widths = [a.shape[1] for a in full] + [part] * len(parts)
    total, count, n = sum(widths), len(places), len(widths)

    def kernel(at_ref, *refs):
        for k, out in enumerate(refs[n:]):

            @pl.when(pl.program_id(0) == k)
            def _(out=out):
                start = 0
                for source, width in zip(refs[:n], widths):
                    out[:, start : start + width] = source[...]
                    start += width

    return pl.pallas_call(
        kernel,
        grid_spec=pltpu.PrefetchScalarGridSpec(
            num_scalar_prefetch=1,
            grid=(count,),
            in_specs=[whole(*a.shape) for a in full]
            + [pl.BlockSpec((rows, part), lambda k, at: (0, at[k]))] * len(parts),
            out_specs=[whole(rows, total)] * count,
        ),
        out_shape=[jax.ShapeDtypeStruct((rows, total), BF)] * count,
        compiler_params=pltpu.CompilerParams(vmem_limit_bytes=32 * 2**20),
        cost_estimate=COST,
        name="side_by_side",
    )(numbers(places), *full, *parts)


def assemble(pieces, rows, width, done=()):
    arrays = [a.reshape(-1, a.shape[-1]) for a, _, _ in pieces]
    counts = [a.shape[0] // LANES for a in arrays]
    firsts = [sum(counts[:k]) for k in range(len(counts))]
    steps = rows // LANES
    at = [o // LANES for _, _, offsets in pieces for o in offsets]

    def kernel(at_ref, *refs):
        step, out = pl.program_id(0), refs[-1]
        for source, first, count in zip(refs, firsts, counts):

            @pl.when((step >= first) & (step < first + count))
            def _(source=source):
                out[...] = source[...]

    def block_of(i):
        return lambda k, at: (jnp.clip(k - firsts[i], 0, counts[i] - 1), at[steps + i])

    return pl.pallas_call(
        kernel,
        grid_spec=pltpu.PrefetchScalarGridSpec(
            num_scalar_prefetch=1,
            grid=(steps,),
            in_specs=[pl.BlockSpec((LANES, width), block_of(i)) for i in range(len(arrays))]
            + [pl.BlockSpec(memory_space=pl.ANY)] * len(done),
            out_specs=pl.BlockSpec((LANES, width), lambda k, at: (at[k], 0)),
        ),
        out_shape=jax.ShapeDtypeStruct((rows, width), arrays[0].dtype),
        compiler_params=pltpu.CompilerParams(vmem_limit_bytes=32 * 2**20),
        cost_estimate=COST,
        name="assemble",
    )(numbers(at + [column for _, column, _ in pieces]), *arrays, *done)


def lay_both(pieces, at, proj_rows, fc_rows, count):
    steps = len(at)
    per = steps // 2
    columns = pieces[0].shape[-1]

    def kernel(at_ref, *refs):
        step = pl.program_id(0)
        proj_out, fc_out = refs[-2:]
        for k in range(steps):
            fc_ref = refs[(per + 1) * (k // per)]
            proj_ref = refs[(per + 1) * (k // per) + 1 + k % per]

            @pl.when(step == k)
            def _(fc_ref=fc_ref, proj_ref=proj_ref):
                part = proj_rows // 2
                for x in (0, 1):
                    for h in (0, 1):
                        proj_out[part * x : part * (x + 1), columns * h : columns * (h + 1)] = (
                            proj_ref[x, part * h : part * (h + 1)].astype(F32)
                        )
                    for j in range(count):
                        start = columns * (2 * j + x)
                        fc_out[:, start : start + columns] = fc_ref[
                            x, 0, fc_rows * j : fc_rows * (j + 1)
                        ].astype(F32)

    fc_rows_all = count * fc_rows

    def fc_block(i):
        return pl.BlockSpec(
            (2, 1, fc_rows_all, columns),
            lambda k, at: (0, jnp.clip(k - i * per, 0, per - 1), 0, 0),
        )

    specs = []
    for i in (0, 1):
        specs += [fc_block(i)] + [whole(*p.shape) for p in pieces[1 : per + 1]]
    shapes = [(proj_rows, 2 * columns), (fc_rows, 2 * count * columns)]
    return pl.pallas_call(
        kernel,
        grid_spec=pltpu.PrefetchScalarGridSpec(
            num_scalar_prefetch=1,
            grid=(steps,),
            in_specs=specs,
            out_specs=[pl.BlockSpec(shape, lambda k, at: (at[k], 0)) for shape in shapes],
        ),
        out_shape=[jax.ShapeDtypeStruct((steps * n, width), F32) for n, width in shapes],
        compiler_params=pltpu.CompilerParams(vmem_limit_bytes=56 * 2**20),
        cost_estimate=COST,
        name="lay_both",
    )(numbers(at), *pieces)


def add_cut(arrays, view, block, places):
    count, dims = len(places), len(view)

    def kernel(at_ref, *refs):
        total = functools.reduce(jnp.add, [r[...].astype(F32) for r in refs[: len(arrays)]])
        for k, out in enumerate(refs[len(arrays) :]):

            @pl.when(pl.program_id(0) == k)
            def _(out=out):
                out[...] = total.astype(BF)

    def index(k, at):
        return tuple(at[k * dims + i] for i in range(dims))

    return pl.pallas_call(
        kernel,
        grid_spec=pltpu.PrefetchScalarGridSpec(
            num_scalar_prefetch=1,
            grid=(count,),
            in_specs=[pl.BlockSpec(block, index)] * len(arrays),
            out_specs=[whole(*block)] * count,
        ),
        out_shape=[jax.ShapeDtypeStruct(block, BF)] * count,
        compiler_params=pltpu.CompilerParams(vmem_limit_bytes=40 * 2**20),
        cost_estimate=COST,
        name="add_cut",
    )(numbers([i for place in places for i in place]), *[a.reshape(view) for a in arrays])


def laid_out(mine, theirs, core, shapes, cut):
    count, rows, width = mine.shape

    def kernel(core_ref, mine_ref, theirs_ref, *outs):
        def write(piece):
            for out, value in zip(outs, cut(piece.astype(F32))):
                out[...] = value

        step = pl.program_id(0)

        @pl.when(step < count)
        def _():
            write(mine_ref[0])

        @pl.when(step >= count)
        def _():
            write(theirs_ref[0])

    def out_block(k, core_ref):
        own = (k < count).astype(jnp.int32)
        return (jnp.where(core_ref[0] == own, 1 - 0 * k, 0 * k) * count + k % count, 0)

    return pl.pallas_call(
        kernel,
        grid_spec=pltpu.PrefetchScalarGridSpec(
            num_scalar_prefetch=1,
            grid=(2 * count,),
            in_specs=[
                pl.BlockSpec((1, rows, width), lambda k, r: (jnp.minimum(k, count - 1), 0, 0)),
                pl.BlockSpec((1, rows, width), lambda k, r: (jnp.maximum(k - count, 0), 0, 0)),
            ],
            out_specs=[pl.BlockSpec(shape, out_block) for shape in shapes],
        ),
        out_shape=[
            jax.ShapeDtypeStruct((2 * count * n, columns), F32) for n, columns in shapes
        ],
        compiler_params=pltpu.CompilerParams(vmem_limit_bytes=32 * 2**20),
        cost_estimate=COST,
        name="laid_out",
    )(core.reshape(1).astype(jnp.int32), mine, theirs)


def matmul(left, right):
    return jnp.dot(left, right, preferred_element_type=F32)


def tall(left, right):
    return lax.dot_general(left, right, (((0,), (0,)), ((), ())), preferred_element_type=F32)


def wide(left, right):
    return lax.dot_general(left, right, (((1,), (1,)), ((), ())), preferred_element_type=F32)


def gelu_tanh(values):
    return jax.nn.gelu(values, approximate=True)


def whole(*shape):
    return pl.BlockSpec(shape, lambda *_: (0,) * len(shape))


def dot_wide(left, right):
    return lax.dot_general(left, right, (((1,), (1,)), ((), ())), preferred_element_type=F32)


def per_head(ref, first, count):
    return jnp.concatenate(
        [ref[first : first + count, k : k + LANES] for k in range(0, ref.shape[1], LANES)]
    )


def masked_scores(keys, queries, places, own, begin, step):
    scores = dot_wide(keys, queries)
    places = jnp.concatenate([places, places], axis=1)
    below = scores.shape[0] - step
    parts = []
    if below:
        parts.append(jnp.where(places[:below] >= begin, scores[:below], MASKED))
    near = (places[below:] >= begin) & (places[below:] <= own)
    parts.append(jnp.where(near, scores[below:], MASKED))
    return jnp.concatenate(parts) if below else parts[0]


def attend(q, kv, values_t, places, own, begin, scale, done=()):
    rows, width = q.shape
    groups = own.shape[0]
    part, step = rows // groups, kv.shape[0] // groups
    factor = scale * math.log2(math.e)

    def kernel(q_ref, kv_ref, vt_ref, place_ref, own_ref, begin_ref, *refs):
        out_ref, log_ref, top_ref = refs[len(done) :]
        for j in range(groups):
            n, row = step * (j + 1), slice(j, j + 1)
            scores = masked_scores(
                kv_ref[:n, :LANES],
                per_head(q_ref, part * j, part),
                place_ref[:n, :],
                own_ref[row, :],
                begin_ref[row, :],
                step,
            )
            top = jnp.max(scores, axis=0, keepdims=True)
            power = jnp.exp2((scores - top) * factor)
            total = jnp.sum(power, axis=0, keepdims=True)
            probs = (power * (1.0 / total)).astype(BF)
            out = jnp.dot(vt_ref[:, :n], probs, preferred_element_type=F32).T
            for k in range(width // LANES):
                out_ref[part * j : part * (j + 1), k * LANES : (k + 1) * LANES] = out[
                    part * k : part * (k + 1)
                ].astype(BF)
            log_ref[row, :] = top * factor + jnp.log2(total)
            top_ref[row, :] = top

    return pl.pallas_call(
        kernel,
        in_specs=[pl.BlockSpec(memory_space=pltpu.VMEM)] * 6
        + [pl.BlockSpec(memory_space=pl.ANY)] * len(done),
        out_shape=[
            jax.ShapeDtypeStruct((rows, width), BF),
            jax.ShapeDtypeStruct(own.shape, F32),
            jax.ShapeDtypeStruct(own.shape, F32),
        ],
        compiler_params=pltpu.CompilerParams(vmem_limit_bytes=48 * 2**20),
        cost_estimate=BRIEF,
        name="attend",
    )(q, kv, values_t, places, own, begin, *done)


def attend_back(q, grad, kv, keys_t, places, own, begin, logs, scale, done=()):
    rows, width = q.shape
    total = kv.shape[0]
    groups = own.shape[0]
    part, step = rows // groups, total // groups
    factor = scale * math.log2(math.e)

    def kernel(
        q_ref, g_ref, kv_ref, kt_ref, place_ref, own_ref, begin_ref, log_ref, *refs
    ):
        dq_ref, dkv_ref, acc_ref = refs[len(done) :]
        for j in reversed(range(groups)):
            n, row = step * (j + 1), slice(j, j + 1)
            queries = per_head(q_ref, part * j, part)
            grads = per_head(g_ref, part * j, part)
            scores = masked_scores(
                kv_ref[:n, :LANES],
                queries,
                place_ref[:n, :],
                own_ref[row, :],
                begin_ref[row, :],
                step,
            )
            prob = jnp.exp2(scores * factor - log_ref[row, :])
            dprob = dot_wide(kv_ref[:n, LANES:], grads)
            inner = jnp.sum(prob * dprob, axis=0, keepdims=True)
            dscores = (prob * (dprob - inner)).astype(BF)
            dq = jnp.dot(kt_ref[:, :n], dscores, preferred_element_type=F32).T * scale
            for k in range(width // LANES):
                dq_ref[part * j : part * (j + 1), k * LANES : (k + 1) * LANES] = dq[
                    part * k : part * (k + 1)
                ].astype(BF)
            dkeys = jnp.dot(dscores, queries, preferred_element_type=F32)
            dvalues = jnp.dot(prob.astype(BF), grads, preferred_element_type=F32)
            if j == groups - 1:
                acc_ref[:, :LANES] = dkeys
                acc_ref[:, LANES:] = dvalues
            else:
                acc_ref[:n, :LANES] += dkeys
                acc_ref[:n, LANES:] += dvalues
        dkv_ref[:, :LANES] = (acc_ref[:, :LANES] * scale).astype(BF)
        dkv_ref[:, LANES:] = acc_ref[:, LANES:].astype(BF)

    return pl.pallas_call(
        kernel,
        in_specs=[pl.BlockSpec(memory_space=pltpu.VMEM)] * 8
        + [pl.BlockSpec(memory_space=pl.ANY)] * len(done),
        out_shape=[
            jax.ShapeDtypeStruct((rows, width), BF),
            jax.ShapeDtypeStruct(kv.shape, BF),
        ],
        scratch_shapes=[pltpu.VMEM(kv.shape, F32)],
        compiler_params=pltpu.CompilerParams(vmem_limit_bytes=48 * 2**20),
        cost_estimate=COST,
        name="attend_back",
    )(q, grad, kv, keys_t, places, own, begin, logs, *done)


def feed_forward(h, dy, w_fc, b_fc, w_proj, parts):
    tokens, width = h.shape
    units, part, rows = w_fc.shape[1], 512, tokens // parts
    curve = math.sqrt(2.0 / math.pi)

    def kernel(h_ref, dy_ref, fc_ref, b_ref, proj_ref, *refs):
        g_ref, du_ref, sum_ref, *dh_refs, acc_ref = refs
        step = pl.program_id(0)
        u = jnp.dot(h_ref[...], fc_ref[...], preferred_element_type=F32) + b_ref[...]
        dg = dot_wide(dy_ref[...], proj_ref[...])
        square = u * u
        bend = jnp.tanh(curve * u * (1.0 + 0.044715 * square))
        half = 0.5 + 0.5 * bend
        g_ref[...] = (u * half).astype(BF)
        slope = half + 0.5 * curve * u * (1.0 - bend * bend) * (1.0 + 3 * 0.044715 * square)
        du = (dg * slope).astype(BF)
        du_ref[...] = du
        sum_ref[...] = jnp.sum(du.astype(F32), axis=0, keepdims=True)
        term = dot_wide(du, fc_ref[...])

        @pl.when(step == 0)
        def _():
            acc_ref[...] = term

        @pl.when(step > 0)
        def _():
            acc_ref[...] += term

        @pl.when(step == units // part - 1)
        def _():
            for k, dh_ref in enumerate(dh_refs):
                dh_ref[...] = acc_ref[k * rows : (k + 1) * rows, :].astype(BF)

    along = lambda k: (0, k)
    return pl.pallas_call(
        kernel,
        grid=(units // part,),
        in_specs=[
            whole(tokens, width),
            whole(tokens, width),
            pl.BlockSpec((width, part), along),
            pl.BlockSpec((1, part), along),
            pl.BlockSpec((part, width), lambda k: (k, 0)),
        ],
        out_specs=[
            pl.BlockSpec((tokens, part), along),
            pl.BlockSpec((tokens, part), along),
            pl.BlockSpec((1, part), along),
            *[whole(rows, width)] * parts,
        ],
        out_shape=[
            jax.ShapeDtypeStruct((tokens, units), BF),
            jax.ShapeDtypeStruct((tokens, units), BF),
            jax.ShapeDtypeStruct((1, units), F32),
            *[jax.ShapeDtypeStruct((rows, width), BF)] * parts,
        ],
        scratch_shapes=[pltpu.VMEM((tokens, width), F32)],
        compiler_params=pltpu.CompilerParams(vmem_limit_bytes=56 * 2**20),
        cost_estimate=COST,
        name="feed_forward",
    )(h, dy, w_fc, b_fc.reshape(1, units), w_proj)


def products(pairs, at_left, at_right, extra=None, split=False):
    outs, per = len(at_left), len(at_left[0])
    tokens = pairs[0][0].shape[0]
    widths = [w for _, _, w in pairs]
    n, total = len(pairs), sum(widths)
    rows = per * LANES

    def kernel(at_ref, *refs):
        values, start = [], 0
        for i, width in enumerate(widths):
            own = refs[i * (per + 1) : (i + 1) * (per + 1)]
            left = jnp.concatenate([r[...] for r in own[:per]], axis=1)
            value = lax.dot_general(
                left, own[per][...], (((0,), (0,)), ((), ())), preferred_element_type=F32
            )
            if extra is not None:
                value = value + refs[n * (per + 1)][:, start : start + width].astype(F32)
            values.append(value.astype(BF))
            start += width

        def write(out):
            start = 0
            for value, width in zip(values, widths):
                out[:, start : start + width] = value
                start += width

        for k, out in enumerate(refs[n * (per + 1) + (extra is not None) :]):
            if split:
                pl.when(pl.program_id(0) == k)(functools.partial(write, out))
            else:
                write(out)

    def left_block(j):
        return lambda k, at: (0, at[k * per + j])

    def right_block(k, at):
        return (0, at[outs * per + k])

    specs, operands = [], []
    for left, right, width in pairs:
        specs += [pl.BlockSpec((tokens, LANES), left_block(j)) for j in range(per)]
        specs.append(pl.BlockSpec((tokens, width), right_block))
        operands += [left] * per + [right]
    if extra is not None:
        specs.append(pl.BlockSpec((rows, total), lambda k, at: (k, 0)))
        operands.append(extra)
    if split:
        out_specs = [whole(rows, total)] * outs
        out_shape = [jax.ShapeDtypeStruct((rows, total), BF)] * outs
    else:
        out_specs = [pl.BlockSpec((rows, total), lambda k, at: (k, 0))]
        out_shape = [jax.ShapeDtypeStruct((outs * rows, total), BF)]
    return pl.pallas_call(
        kernel,
        grid_spec=pltpu.PrefetchScalarGridSpec(
            num_scalar_prefetch=1, grid=(outs,), in_specs=specs, out_specs=out_specs
        ),
        out_shape=out_shape,
        compiler_params=pltpu.CompilerParams(vmem_limit_bytes=56 * 2**20),
        cost_estimate=COST,
        name="products",
    )(numbers([i for row in at_left for i in row] + list(at_right)), *operands)


def norm_parts(values):
    centered = values - jnp.mean(values, axis=-1, keepdims=True)
    rate = lax.rsqrt(jnp.mean(centered * centered, axis=-1, keepdims=True) + EPSILON)
    return centered * rate, rate


def norm_back(grad, gain, hat, rate):
    e = grad * gain
    inner = jnp.mean(e * hat, axis=-1, keepdims=True)
    return rate * (e - jnp.mean(e, axis=-1, keepdims=True) - hat * inner)


def shards(
    hidden,
    cotangent,
    lengths,
    source_pos,
    owner_slot,
    ln1_gain,
    ln1_bias,
    query_weight,
    query_bias,
    kv_weight,
    value_bias,
    out_weight,
    out_bias,
    ln2_gain,
    ln2_bias,
    fc_weight,
    fc_bias,
    proj_weight,
    proj_bias,
):
    rows, width = hidden.shape
    ny, nz, nctx = lax.axis_size(Y), lax.axis_size(Z), lax.axis_size(CONTEXT)
    y, xl, z, c = (lax.axis_index(a) for a in (Y, XL, Z, CORE))
    xo, co = 1 - xl, 1 - c
    ctx = lax.axis_index(CONTEXT)
    sub = rows // nctx
    head = kv_weight.shape[1] // 2
    heads = width // head
    scale = 1.0 / math.sqrt(head)
    shard = query_weight.shape[0]
    nzx = lax.axis_size(ZX)
    half = shard // 2
    ff = proj_weight.shape[0]
    block = 2 * ff

    small = jnp.concatenate(
        [
            jnp.stack([ln1_gain, ln1_bias, query_bias, out_bias, ln2_gain, ln2_bias, proj_bias]),
            jnp.pad(value_bias, (0, shard - value_bias.shape[0]))[None],
            fc_bias.reshape(-1, shard),
            jnp.zeros((4, shard), BF),
        ]
    )
    first = pack(
        [small, kv_weight],
        [out_weight, fc_weight],
        [lambda k: (c, z), lambda k: (c, k // 2 * nz + z)],
    )
    first = lax.all_to_all(first, FSDP, 0, 0, tiled=True)
    small = first[:, :16]
    gain1, bias1, bq, bo, gain2, bias2, bproj = (
        small[:, k].reshape(width).astype(F32) for k in range(7)
    )
    bv = small[:, 7, : value_bias.shape[0]].reshape(head).astype(F32)
    bfc = pick(small[:, 8:12].reshape(ny, block), y, 0).astype(F32)
    wkv = first[:, 16 : 16 + shard].reshape(width, 2 * head)

    q_mine = lax.all_to_all(
        repeat_block(query_weight, c, 2 * ny, (first,)), FSDP, 0, 0, tiled=True
    )

    def quarters(piece):
        return [piece] + [shift(piece, Z, d) for d in range(1, nz)]

    def whole_weight(mine, theirs, cost):
        there = [(z - d) % nz for d in range(nz)]
        return assemble_quarters(
            mine + theirs, [(c, k) for k in there] + [(co, k) for k in there], cost
        )

    at = 16 + shard
    o_mine = quarters(first[:, at : at + shard])

    x = hidden.astype(F32)
    hat1, rate1 = norm_parts(x)
    h1 = (hat1 * gain1 + bias1).astype(BF)
    kv = matmul(h1, wkv) + jnp.concatenate([jnp.zeros((head,), F32), bv])
    owned = lax.dynamic_slice_in_dim(owner_slot[0], ctx * rows, rows)
    target = owned // rows * sub + owned % rows - ctx * sub
    deal = (target[:, None] == jnp.arange(rows, dtype=jnp.int32)[None, :]).astype(BF)

    def dealt(array):
        pieces = array.astype(BF).reshape(nctx, sub, width)
        return lax.all_to_all(pieces, CONTEXT, 0, 0, tiled=True).reshape(rows, width)

    dealing = tall(deal, cotangent).astype(BF).reshape(nctx, -1, 2 * head)
    kv, q_mine, o_mine, dealing = gate((kv.astype(BF), q_mine, o_mine, dealing))
    q_theirs, o_theirs = swap(q_mine, CORE), [swap(m, CORE) for m in o_mine]
    kv = jnp.broadcast_to(kv[None], (nctx, rows, 2 * head))
    all_kv = lax.all_to_all(jnp.concatenate([kv, dealing], axis=1), CONTEXT, 0, 0, tiled=True)
    shards_at = [shard * k for k in range(2 * ny)]
    wq = assemble(
        [
            (q_mine, 0, [a + half * c for a in shards_at]),
            (q_theirs, 0, [a + half * co for a in shards_at]),
        ],
        width,
        width,
    )
    all_kv, wq, o_mine, o_theirs, proj_weight, first = gate(
        (all_kv, wq, o_mine, o_theirs, proj_weight, first)
    )
    dy = all_kv[:, rows:].reshape(rows, width)
    all_kv = all_kv[:, :rows]
    f_mine = quarters(first[:, at + shard :])
    p_mine = swap(lax.dynamic_slice_in_dim(proj_weight, ff // 2 * c, ff // 2), XL)
    wo = whole_weight(o_mine, o_theirs, BRIEF)
    q = (matmul(h1, wq) + bq).astype(BF)

    positions = source_pos[0]
    starts = jnp.cumsum(lengths[0]) - lengths[0]
    own_pos = lax.dynamic_slice_in_dim(positions, ctx * rows, rows)
    seq_start = jnp.max(jnp.where(starts[None, :] <= own_pos[:, None], starts[None, :], 0), axis=1)
    groups = rows // 16
    natural = jnp.moveaxis(all_kv.reshape(nctx, nctx, sub, 2 * head), 0, 1)
    natural = natural.reshape(nctx * rows, 2 * head)
    xh = lax.axis_index(XH)
    places = jnp.moveaxis(positions.reshape(nctx, nctx, sub), 0, 1).reshape(nctx * rows, 1)
    places = jnp.broadcast_to(places, (nctx * rows, LANES))

    def for_heads(array):
        array = jnp.broadcast_to(array.reshape(groups, 1, 16), (groups, heads, 16))
        return array.reshape(groups, heads * 16)

    own, begin = for_heads(own_pos), for_heads(seq_start)
    attended, logs, tops = attend(
        q, natural, natural[:, head:].T, places, own, begin, scale
    )
    local_max = jnp.max(tops.reshape(groups, heads, 16), axis=(0, 2)) * scale

    def pieces_of(array):
        return [array] + [shift(array, Y, d) for d in range(1, ny)]

    dy_pieces = pieces_of(dy)
    attended, wo, f_mine, dy_pieces, p_mine = gate((attended, wo, f_mine, dy_pieces, p_mine))
    x2 = x + matmul(attended, wo) + bo
    hat2, rate2 = norm_parts(x2)
    h2 = (hat2 * gain2 + bias2).astype(BF)

    def over_y(array):
        return jnp.concatenate(pieces_of(array))

    h2, f_mine, p_mine = gate((h2, f_mine, p_mine))
    dy_all = jnp.concatenate(dy_pieces)
    h2_pieces = pieces_of(h2)
    wfc = whole_weight(f_mine, [swap(m, CORE) for m in f_mine], COST)
    p_theirs = swap(p_mine, CORE)
    wproj = assemble(
        [
            (proj_weight, 0, [ff * xl + LANES * k for k in range(ff // LANES)]),
            (p_mine, 0, [ff * xo + ff // 2 * c + LANES * k for k in range(ff // 2 // LANES)]),
            (p_theirs, 0, [ff * xo + ff // 2 * co + LANES * k for k in range(ff // 2 // LANES)]),
        ],
        block,
        width,
    )
    h2_pieces, wfc, wproj = gate((h2_pieces, wfc, wproj))
    h2_all = jnp.concatenate(h2_pieces)
    g, du, du_sum, *dh2 = feed_forward(h2_all, dy_all, wfc, bfc, wproj, ny)

    x_ring = [(a, b) for a in (0, 1) for b in (0, 1)]
    zs = [(z + d) % nz for d in range(nz)]
    part_z = half // nz

    def flip(array, a, b):
        moves = [(2 * i + j, 2 * (i ^ a) + (j ^ b)) for i in (0, 1) for j in (0, 1)]
        return lax.ppermute(array, (XL, XH), moves)

    def over_x(parts):
        return [parts[0]] + [flip(p, a, b) for p, (a, b) in zip(parts[1:], x_ring[1:])]

    def over_z(parts):
        return [parts[0]] + [shift(parts[d], Z, d) for d in range(1, nz)]

    def core_summed(pairs, left_at, right_at):
        (theirs,) = products(pairs, left_at(co), right_at)
        return products(pairs, left_at(c), right_at, swap(theirs, CORE), True)

    dproj = core_summed(
        [(g, dy_all, width)],
        lambda core: [[(k * 2 + core) * nz + there for k in (0, 1)] for there in zs],
        [0] * nz,
    )
    dh2 = [dh2[0]] + [shift(dh2[d], Y, -d) for d in range(1, ny)]
    dh2, dproj, attended, h1 = gate((dh2, dproj, attended, h1))
    dproj = over_z(dproj)
    sent = side_by_side([], [attended, h1], [(y + d) % ny for d in range(ny)])
    sent = [sent[0]] + [shift(sent[d], Y, d) for d in range(1, ny)]
    dh2 = functools.reduce(jnp.add, [t.astype(F32) for t in dh2])

    dy_f = dy.astype(F32)
    dx2 = dy_f + norm_back(dh2, gain2, hat2, rate2)
    da = dx2.astype(BF)

    dattended = wide(da, wo).astype(BF)
    dq, dkv = attend_back(
        q, dattended, natural, natural[:, :head].T, places, own, begin, logs, scale
    )
    dfc = core_summed(
        [(h2_all, du, block // 2)],
        lambda core: [[(k * 2 + (xl ^ a)) * 2 + core for k in range(ny)] for a, _ in x_ring],
        [xh ^ b for _, b in x_ring],
    )
    result_terms = matmul(g, wproj).astype(BF)
    dq, dkv, da, dproj, dfc, result_terms, sent = gate(
        (dq, dkv, da, dproj, dfc, result_terms, sent)
    )
    dfc = over_x(dfc)
    sent = jnp.concatenate(sent)
    attended_columns, h1_columns = sent[:, : block // ny], sent[:, block // ny :]
    dkv = jnp.moveaxis(dkv.reshape(nctx, nz, 2, 2, sub, 2 * head), 0, 3)
    dkv = dkv.reshape(nz, 2, 2, rows, 2 * head)

    def plus(mine, *got):
        return functools.reduce(jnp.add, [t.astype(F32) for t in (mine, *got)]).astype(BF)

    dkv = plus(pick(dkv, c, 2), swap(pick(dkv, co, 2), CORE))
    dkv = plus(pick(dkv, xh, 1), swap(pick(dkv, 1 - xh, 1), XH))
    dkv = plus(pick(dkv, z, 0), *[shift(pick(dkv, k, 0), Z, d) for d, k in list(enumerate(zs))[1:]])
    da_dq = over_y(jnp.concatenate([da, dq], axis=1))

    dproj, dfc, da_dq, dkv, result_terms, dq = gate(
        (dproj, dfc, da_dq, dkv, result_terms, dq)
    )
    dh1 = wide(dq, wq)
    dproj = add_cut(
        dproj,
        (2, 2, half // 2, width),
        (1, 1, half // 2, width),
        [(xl ^ a, xh ^ b, 0, 0) for a, b in x_ring],
    )
    dproj = over_x(dproj)
    dfc = add_cut(
        dfc,
        (ny, nz, part_z, block // 2),
        (ny, 1, part_z, block // 2),
        [(0, there, 0, 0) for there in zs],
    )
    dfc = over_z(dfc)
    dkv_all = over_y(dkv)
    part_fc = half // nzx

    def spread(terms):
        terms = terms.reshape(2 * nzx, part_fc, -1)
        return lax.all_to_all(terms, (XL,) + ZX, 0, 0, tiled=True)

    da_all, dq_all = da_dq[:, :width], da_dq[:, width:]
    (theirs,) = products([(attended_columns, da_all, width)], [[co, 2 + co]], [0])
    (dwo,) = products(
        [(attended_columns, da_all, width)], [[c, 2 + c]], [0], swap(theirs, CORE)
    )
    dwo = spread(dwo)
    result = result_terms.reshape(ny, rows, width)
    result = [result[0]] + [shift(result[d], Y, -d) for d in range(1, ny)]
    dproj, dfc, dkv_all, result, dh1, dwo = gate((dproj, dfc, dkv_all, result, dh1, dwo))
    dproj = add_cut(
        dproj,
        (half // 2, width),
        (half // 2, width // 2),
        [(0, 0), (0, 1)],
    )
    dproj = jnp.concatenate(dproj)
    dproj_other = swap(dproj, XH)
    dfc = add_cut(
        dfc,
        (ny, part_z, block // 2),
        (1, part_z, block // 2),
        [((y + d) % ny, 0, 0) for d in range(ny)],
    )
    dfc = [dfc[0]] + [shift(dfc[d], Y, d) for d in range(1, ny)]
    dfc, dproj, dproj_other = gate((dfc, dproj, dproj_other))
    dfc = jnp.stack(dfc)

    dfc = jnp.concatenate([pick(dfc, (y - k) % ny, 0)[0] for k in range(ny)])
    there = [(z - d) % nz for d in range(nz)]
    dfc = [dfc] + [shift(dfc, Z, d) for d in range(1, nz)]
    pairs = [(h1_columns, dq_all, width), (h1_columns, dkv_all, 2 * head)]
    (theirs,) = products(pairs, [[co, 2 + co]], [0])
    (dwq,) = products(pairs, [[c, 2 + c]], [0], swap(theirs, CORE))
    dh1 = dh1 + wide(dkv, wkv)
    grad_hidden = (dx2 + norm_back(dh1, gain1, hat1, rate1)).astype(BF)
    result = functools.reduce(jnp.add, [t.astype(F32) for t in result])
    result = dealt((x2 + result + bproj).astype(BF))
    def total(array):
        return jnp.sum(array.astype(F32), axis=0)

    vectors = [
        total(dy),
        total(dh2 * hat2),
        total(dh2),
        total(da),
        total(dq),
        total(dh1 * hat1),
        total(dh1),
    ]
    vectors = [v.reshape(2 * ny, 1, shard) for v in vectors]
    du_sum = du_sum.reshape(1, 2, ff // shard, shard)
    du_sum = lax.dynamic_update_slice(
        jnp.zeros((ny, 2, ff // shard, shard), F32), du_sum, (y, 0, 0, 0)
    )
    bv_sum = total(dkv[:, head:]).reshape(2 * ny, 1, -1)
    top_high = lax.reduce_precision(local_max, 8, 7)
    tops = jnp.concatenate([top_high, local_max - top_high])
    tops = jnp.broadcast_to(tops, (2 * ny, 1, 2 * heads))
    last = [jnp.pad(v, ((0, 0), (0, 0), (0, shard - v.shape[2]))) for v in (bv_sum, tops)]
    vectors += [du_sum.reshape(2 * ny, -1, shard), *last]
    joined = jnp.concatenate(vectors, axis=1).astype(BF)
    joined = jnp.pad(joined, ((0, 0), (0, 16 - joined.shape[1]), (0, 0)))
    joined = jnp.broadcast_to(joined[:, None], (2 * ny, nctx, *joined.shape[1:]))
    joined = joined.reshape(-1, 16, shard)
    joined = lax.all_to_all(joined, EVERY, 0, 0, tiled=True)
    dfc, dwq, dwo, dproj, dproj_other, result, joined = gate(
        (dfc, dwq, dwo, dproj, dproj_other, result, joined)
    )
    output = matmul(deal, result).astype(BF)

    dfc = jnp.stack(dfc)
    dfc_other = swap(dfc, XH)
    dproj = pair(dproj, dproj_other, xh)
    dproj = [dproj] + [shift(dproj, Z, d) for d in range(1, nz)]
    small_w = jnp.concatenate([dwo, spread(dwq)], axis=2)
    dfc, dfc_other, dproj, small_w = gate((dfc, dfc_other, dproj, small_w))
    small_w = copies(jnp.sum(small_w.astype(F32), axis=0).astype(BF), ZX)
    dfc = pair(dfc, dfc_other, xh)
    mine = [dfc] + dproj
    mine = mine + [swap(m, CORE) for m in mine]
    grad_proj_w, grad_fc_w = lay_both(
        mine,
        [c * nz + k for k in there] + [co * nz + k for k in there],
        half,
        part_z,
        ny,
    )
    small_w, grad_proj_w, grad_fc_w = gate((small_w, grad_proj_w, grad_fc_w))
    grad_out_w, grad_query_w, grad_kv_w = laid_out(
        small_w,
        swap(small_w, CORE),
        c,
        [(part_fc, width), (part_fc, width), (part_fc, 2 * head)],
        lambda piece: (piece[:, :width], piece[:, width : 2 * width], piece[:, 2 * width :]),
    )

    tops = joined[:, 12].astype(F32)
    maxima = jnp.max(tops[:, :heads] + tops[:, heads : 2 * heads], axis=0)
    joined = jnp.sum(joined.astype(F32), axis=0)
    g_bproj, g_gain2, g_bias2, g_bo, g_bq, g_gain1, g_bias1 = (joined[k] for k in range(7))
    g_bfc, g_bv = joined[7:11].reshape(ff), joined[11, : value_bias.shape[0]]

    clip_ratio = CLIP_LIMIT / jnp.maximum(maxima, CLIP_LIMIT)
    column_scale = jnp.repeat(jnp.sqrt(clip_ratio), head)
    clipped_qw = query_weight.astype(F32) * column_scale[None, :]
    clipped_qb = query_bias.astype(F32) * lax.dynamic_slice_in_dim(
        column_scale, lax.axis_index(FSDP) * shard, shard
    )
    clipped_kw = kv_weight[:, :head].astype(F32) * jnp.sqrt(jnp.min(clip_ratio))
    return (
        output,
        grad_hidden,
        g_gain1,
        g_bias1,
        grad_query_w,
        g_bq,
        grad_kv_w,
        g_bv,
        grad_out_w,
        g_bo,
        g_gain2,
        g_bias2,
        grad_fc_w,
        g_bfc,
        grad_proj_w,
        g_bproj,
        maxima,
        clipped_qw,
        clipped_qb,
        clipped_kw,
    )


def solution(mesh):
    torus = Mesh(mesh.devices.reshape(4, 2, 4, 2, 2), EVERY)
    tokens, table, vector, matrix = P(EVERY, None), P(FSDP, None), P(FSDP), P(FSDP, None)
    return jax.shard_map(
        shards,
        mesh=torus,
        in_specs=(
            tokens,
            tokens,
            table,
            table,
            table,
            vector,
            vector,
            matrix,
            vector,
            matrix,
            vector,
            matrix,
            vector,
            vector,
            vector,
            matrix,
            vector,
            matrix,
            vector,
        ),
        out_specs=(
            tokens,
            tokens,
            vector,
            vector,
            matrix,
            vector,
            matrix,
            vector,
            matrix,
            vector,
            vector,
            vector,
            matrix,
            vector,
            matrix,
            vector,
            P(),
            matrix,
            vector,
            matrix,
        ),
        check_vma=False,
    )
```

```python
import functools
import math

import jax
import jax.numpy as jnp
from jax import lax
from jax.experimental import pallas as pl
from jax.experimental.pallas import tpu as pltpu
from jax.sharding import Mesh
from jax.sharding import PartitionSpec as P

Y, XL, Z, XH, CORE = ("fsdp_0", "fsdp_1", "context_0", "context_1", "context_2")
FSDP = (Y, XL)
CONTEXT = (Z, XH, CORE)
ZX = (Z, XH)
EVERY = (Y, XL, Z, XH, CORE)

EPSILON = 1e-05
CLIP_LIMIT = 4.0
MASKED = -1e30
LANES = 128
BRIEF = pl.CostEstimate(flops=0, bytes_accessed=1024, transcendentals=0)
COST = pl.CostEstimate(flops=30_000_000_000, bytes_accessed=1024, transcendentals=0)
BF = jnp.bfloat16
F32 = jnp.float32


def shift(array, axis, by):
    n = lax.axis_size(axis)
    return lax.ppermute(array, axis, [(i, (i + by) % n) for i in range(n)])


def swap(array, axis):
    return shift(array, axis, 1)


def copies(array, axis):
    n = lax.axis_size(axis)
    return lax.all_to_all(jnp.broadcast_to(array[None], (n, *array.shape)), axis, 0, 0, tiled=True)


def gate(values, *done):
    return lax.optimization_barrier((values, done))[0]


def pick(array, index, dim):
    return lax.dynamic_index_in_dim(array, index, dim, keepdims=False)


def pair(own, other, index):
    return jnp.where(index == 0, jnp.stack([own, other]), jnp.stack([other, own]))


def numbers(values):
    return jnp.stack([jnp.asarray(v, jnp.int32) for v in values])


def cut(places, width, done=()):
    arrays = [array for array, _, _ in places]

    def kernel(at_ref, *refs):
        for source, out in zip(refs, refs[len(arrays) + len(done) :]):
            out[...] = source[...]

    def block_of(i):
        return lambda k, at: (at[2 * i], at[2 * i + 1])

    return pl.pallas_call(
        kernel,
        grid_spec=pltpu.PrefetchScalarGridSpec(
            num_scalar_prefetch=1,
            grid=(1,),
            in_specs=[pl.BlockSpec((LANES, width), block_of(i)) for i in range(len(arrays))]
            + [pl.BlockSpec(memory_space=pl.ANY)] * len(done),
            out_specs=[pl.BlockSpec((LANES, width), lambda k, at: (0, 0))] * len(arrays),
        ),
        out_shape=[jax.ShapeDtypeStruct((LANES, width), a.dtype) for a in arrays],
        compiler_params=pltpu.CompilerParams(vmem_limit_bytes=32 * 2**20),
        cost_estimate=COST,
        name="cut",
    )(numbers([n for _, row, column in places for n in (row, column)]), *arrays, *done)


def pack(shared, quarters, where):
    rows = [a.shape[0] for a in shared] + [2 * LANES] * len(quarters)
    wide = shared[0].shape[1]
    count = 8

    def kernel(at_ref, *refs):
        out, start = refs[-1], 0
        for k, length in enumerate(rows):
            if k < len(shared):
                out[0, start : start + length] = refs[k][...]
            else:
                out[0, start : start + LANES] = refs[k][:, :wide]
                out[0, start + LANES : start + length] = refs[k][:, wide:]
            start += length

    def block_of(i):
        return lambda k, at: (at[2 * (i * count + k)], at[2 * (i * count + k) + 1])

    return pl.pallas_call(
        kernel,
        grid_spec=pltpu.PrefetchScalarGridSpec(
            num_scalar_prefetch=1,
            grid=(count,),
            in_specs=[whole(*a.shape) for a in shared]
            + [pl.BlockSpec((LANES, 2 * wide), block_of(i)) for i in range(len(quarters))],
            out_specs=pl.BlockSpec((1, sum(rows), wide), lambda k, at: (k, 0, 0)),
        ),
        out_shape=jax.ShapeDtypeStruct((count, sum(rows), wide), BF),
        compiler_params=pltpu.CompilerParams(vmem_limit_bytes=32 * 2**20),
        cost_estimate=COST,
        name="pack",
    )(numbers([n for by in where for k in range(count) for n in by(k)]), *shared, *quarters)


def repeat_block(array, row, count, done=()):
    width = array.shape[1]

    def kernel(at_ref, in_ref, *refs):
        refs[-1][0] = in_ref[...]

    return pl.pallas_call(
        kernel,
        grid_spec=pltpu.PrefetchScalarGridSpec(
            num_scalar_prefetch=1,
            grid=(count,),
            in_specs=[pl.BlockSpec((LANES, width), lambda k, at: (at[0], 0))]
            + [pl.BlockSpec(memory_space=pl.ANY)] * len(done),
            out_specs=pl.BlockSpec((1, LANES, width), lambda k, at: (k, 0, 0)),
        ),
        out_shape=jax.ShapeDtypeStruct((count, LANES, width), BF),
        compiler_params=pltpu.CompilerParams(vmem_limit_bytes=32 * 2**20),
        cost_estimate=COST,
        name="repeat_block",
    )(numbers([row]), array, *done)


def assemble_quarters(pieces, core_and_z, cost, done=()):
    shards, _, wide = pieces[0].shape
    width = 8 * wide
    steps = 2 * len(pieces)

    def kernel(at_ref, *refs):
        for k, piece in enumerate(refs[: len(pieces)]):

            @pl.when(pl.program_id(0) // 2 == k)
            def _(piece=piece):
                refs[-1][...] = piece[...].reshape(shards, 1, LANES, wide)

    def block_of(i):
        return lambda k, at: (0, jnp.clip(k - 2 * i, 0, 1), 0)

    at = [n for core, z in core_and_z for j in (0, 1) for n in (core, 2 * z + j)]
    return pl.pallas_call(
        kernel,
        grid_spec=pltpu.PrefetchScalarGridSpec(
            num_scalar_prefetch=1,
            grid=(steps,),
            in_specs=[pl.BlockSpec((shards, LANES, wide), block_of(i)) for i in range(len(pieces))]
            + [pl.BlockSpec(memory_space=pl.ANY)] * len(done),
            out_specs=pl.BlockSpec(
                (shards, 1, LANES, wide), lambda k, at: (0, at[2 * k], 0, at[2 * k + 1])
            ),
        ),
        out_shape=jax.ShapeDtypeStruct((shards, 2, LANES, width), BF),
        compiler_params=pltpu.CompilerParams(vmem_limit_bytes=48 * 2**20),
        cost_estimate=cost,
        name="assemble_quarters",
    )(numbers(at), *pieces, *done).reshape(shards * 2 * LANES, width)


def side_by_side(full, parts, places):
    rows = parts[0].shape[0]
    part = 4 * LANES
    widths = [a.shape[1] for a in full] + [part] * len(parts)
    total, count, n = sum(widths), len(places), len(widths)

    def kernel(at_ref, *refs):
        for k, out in enumerate(refs[n:]):

            @pl.when(pl.program_id(0) == k)
            def _(out=out):
                start = 0
                for source, width in zip(refs[:n], widths):
                    out[:, start : start + width] = source[...]
                    start += width

    return pl.pallas_call(
        kernel,
        grid_spec=pltpu.PrefetchScalarGridSpec(
            num_scalar_prefetch=1,
            grid=(count,),
            in_specs=[whole(*a.shape) for a in full]
            + [pl.BlockSpec((rows, part), lambda k, at: (0, at[k]))] * len(parts),
            out_specs=[whole(rows, total)] * count,
        ),
        out_shape=[jax.ShapeDtypeStruct((rows, total), BF)] * count,
        compiler_params=pltpu.CompilerParams(vmem_limit_bytes=32 * 2**20),
        cost_estimate=COST,
        name="side_by_side",
    )(numbers(places), *full, *parts)


def assemble(pieces, rows, width, done=()):
    arrays = [a.reshape(-1, a.shape[-1]) for a, _, _ in pieces]
    counts = [a.shape[0] // LANES for a in arrays]
    firsts = [sum(counts[:k]) for k in range(len(counts))]
    steps = rows // LANES
    at = [o // LANES for _, _, offsets in pieces for o in offsets]

    def kernel(at_ref, *refs):
        step, out = pl.program_id(0), refs[-1]
        for source, first, count in zip(refs, firsts, counts):

            @pl.when((step >= first) & (step < first + count))
            def _(source=source):
                out[...] = source[...]

    def block_of(i):
        return lambda k, at: (jnp.clip(k - firsts[i], 0, counts[i] - 1), at[steps + i])

    return pl.pallas_call(
        kernel,
        grid_spec=pltpu.PrefetchScalarGridSpec(
            num_scalar_prefetch=1,
            grid=(steps,),
            in_specs=[pl.BlockSpec((LANES, width), block_of(i)) for i in range(len(arrays))]
            + [pl.BlockSpec(memory_space=pl.ANY)] * len(done),
            out_specs=pl.BlockSpec((LANES, width), lambda k, at: (at[k], 0)),
        ),
        out_shape=jax.ShapeDtypeStruct((rows, width), arrays[0].dtype),
        compiler_params=pltpu.CompilerParams(vmem_limit_bytes=32 * 2**20),
        cost_estimate=COST,
        name="assemble",
    )(numbers(at + [column for _, column, _ in pieces]), *arrays, *done)


def lay_both(pieces, at, proj_rows, fc_rows, count):
    steps = len(at)
    per = steps // 2
    columns = pieces[0].shape[-1]

    def kernel(at_ref, *refs):
        step = pl.program_id(0)
        proj_out, fc_out = refs[-2:]
        for k in range(steps):
            fc_ref = refs[(per + 1) * (k // per)]
            proj_ref = refs[(per + 1) * (k // per) + 1 + k % per]

            @pl.when(step == k)
            def _(fc_ref=fc_ref, proj_ref=proj_ref):
                part = proj_rows // 2
                for x in (0, 1):
                    for h in (0, 1):
                        proj_out[part * x : part * (x + 1), columns * h : columns * (h + 1)] = (
                            proj_ref[x, part * h : part * (h + 1)].astype(F32)
                        )
                    for j in range(count):
                        start = columns * (2 * j + x)
                        fc_out[:, start : start + columns] = fc_ref[
                            x, 0, fc_rows * j : fc_rows * (j + 1)
                        ].astype(F32)

    fc_rows_all = count * fc_rows

    def fc_block(i):
        return pl.BlockSpec(
            (2, 1, fc_rows_all, columns),
            lambda k, at: (0, jnp.clip(k - i * per, 0, per - 1), 0, 0),
        )

    specs = []
    for i in (0, 1):
        specs += [fc_block(i)] + [whole(*p.shape) for p in pieces[1 : per + 1]]
    shapes = [(proj_rows, 2 * columns), (fc_rows, 2 * count * columns)]
    return pl.pallas_call(
        kernel,
        grid_spec=pltpu.PrefetchScalarGridSpec(
            num_scalar_prefetch=1,
            grid=(steps,),
            in_specs=specs,
            out_specs=[pl.BlockSpec(shape, lambda k, at: (at[k], 0)) for shape in shapes],
        ),
        out_shape=[jax.ShapeDtypeStruct((steps * n, width), F32) for n, width in shapes],
        compiler_params=pltpu.CompilerParams(vmem_limit_bytes=56 * 2**20),
        cost_estimate=COST,
        name="lay_both",
    )(numbers(at), *pieces)


def add_cut(arrays, view, block, places):
    count, dims = len(places), len(view)

    def kernel(at_ref, *refs):
        total = functools.reduce(jnp.add, [r[...].astype(F32) for r in refs[: len(arrays)]])
        for k, out in enumerate(refs[len(arrays) :]):

            @pl.when(pl.program_id(0) == k)
            def _(out=out):
                out[...] = total.astype(BF)

    def index(k, at):
        return tuple(at[k * dims + i] for i in range(dims))

    return pl.pallas_call(
        kernel,
        grid_spec=pltpu.PrefetchScalarGridSpec(
            num_scalar_prefetch=1,
            grid=(count,),
            in_specs=[pl.BlockSpec(block, index)] * len(arrays),
            out_specs=[whole(*block)] * count,
        ),
        out_shape=[jax.ShapeDtypeStruct(block, BF)] * count,
        compiler_params=pltpu.CompilerParams(vmem_limit_bytes=40 * 2**20),
        cost_estimate=COST,
        name="add_cut",
    )(numbers([i for place in places for i in place]), *[a.reshape(view) for a in arrays])


def laid_out(mine, theirs, core, shapes, cut):
    count, rows, width = mine.shape

    def kernel(core_ref, mine_ref, theirs_ref, *outs):
        def write(piece):
            for out, value in zip(outs, cut(piece.astype(F32))):
                out[...] = value

        step = pl.program_id(0)

        @pl.when(step < count)
        def _():
            write(mine_ref[0])

        @pl.when(step >= count)
        def _():
            write(theirs_ref[0])

    def out_block(k, core_ref):
        own = (k < count).astype(jnp.int32)
        return (jnp.where(core_ref[0] == own, 1 - 0 * k, 0 * k) * count + k % count, 0)

    return pl.pallas_call(
        kernel,
        grid_spec=pltpu.PrefetchScalarGridSpec(
            num_scalar_prefetch=1,
            grid=(2 * count,),
            in_specs=[
                pl.BlockSpec((1, rows, width), lambda k, r: (jnp.minimum(k, count - 1), 0, 0)),
                pl.BlockSpec((1, rows, width), lambda k, r: (jnp.maximum(k - count, 0), 0, 0)),
            ],
            out_specs=[pl.BlockSpec(shape, out_block) for shape in shapes],
        ),
        out_shape=[
            jax.ShapeDtypeStruct((2 * count * n, columns), F32) for n, columns in shapes
        ],
        compiler_params=pltpu.CompilerParams(vmem_limit_bytes=32 * 2**20),
        cost_estimate=COST,
        name="laid_out",
    )(core.reshape(1).astype(jnp.int32), mine, theirs)


def matmul(left, right):
    return jnp.dot(left, right, preferred_element_type=F32)


def tall(left, right):
    return lax.dot_general(left, right, (((0,), (0,)), ((), ())), preferred_element_type=F32)


def wide(left, right):
    return lax.dot_general(left, right, (((1,), (1,)), ((), ())), preferred_element_type=F32)


def gelu_tanh(values):
    return jax.nn.gelu(values, approximate=True)


def whole(*shape):
    return pl.BlockSpec(shape, lambda *_: (0,) * len(shape))


def dot_wide(left, right):
    return lax.dot_general(left, right, (((1,), (1,)), ((), ())), preferred_element_type=F32)


def per_head(ref, first, count):
    return jnp.concatenate(
        [ref[first : first + count, k : k + LANES] for k in range(0, ref.shape[1], LANES)]
    )


def masked_scores(keys, queries, places, own, begin, step):
    scores = dot_wide(keys, queries)
    places = jnp.concatenate([places, places], axis=1)
    below = scores.shape[0] - step
    parts = []
    if below:
        parts.append(jnp.where(places[:below] >= begin, scores[:below], MASKED))
    near = (places[below:] >= begin) & (places[below:] <= own)
    parts.append(jnp.where(near, scores[below:], MASKED))
    return jnp.concatenate(parts) if below else parts[0]


def attend(q, kv, values_t, places, own, begin, scale, done=()):
    rows, width = q.shape
    groups = own.shape[0]
    part, step = rows // groups, kv.shape[0] // groups
    factor = scale * math.log2(math.e)

    def kernel(q_ref, kv_ref, vt_ref, place_ref, own_ref, begin_ref, *refs):
        out_ref, log_ref, top_ref = refs[len(done) :]
        for j in range(groups):
            n, row = step * (j + 1), slice(j, j + 1)
            scores = masked_scores(
                kv_ref[:n, :LANES],
                per_head(q_ref, part * j, part),
                place_ref[:n, :],
                own_ref[row, :],
                begin_ref[row, :],
                step,
            )
            top = jnp.max(scores, axis=0, keepdims=True)
            power = jnp.exp2((scores - top) * factor)
            total = jnp.sum(power, axis=0, keepdims=True)
            probs = (power * (1.0 / total)).astype(BF)
            out = jnp.dot(vt_ref[:, :n], probs, preferred_element_type=F32).T
            for k in range(width // LANES):
                out_ref[part * j : part * (j + 1), k * LANES : (k + 1) * LANES] = out[
                    part * k : part * (k + 1)
                ].astype(BF)
            log_ref[row, :] = top * factor + jnp.log2(total)
            top_ref[row, :] = top

    return pl.pallas_call(
        kernel,
        in_specs=[pl.BlockSpec(memory_space=pltpu.VMEM)] * 6
        + [pl.BlockSpec(memory_space=pl.ANY)] * len(done),
        out_shape=[
            jax.ShapeDtypeStruct((rows, width), BF),
            jax.ShapeDtypeStruct(own.shape, F32),
            jax.ShapeDtypeStruct(own.shape, F32),
        ],
        compiler_params=pltpu.CompilerParams(vmem_limit_bytes=48 * 2**20),
        cost_estimate=BRIEF,
        name="attend",
    )(q, kv, values_t, places, own, begin, *done)


def attend_back(q, grad, kv, keys_t, places, own, begin, logs, scale, done=()):
    rows, width = q.shape
    total = kv.shape[0]
    groups = own.shape[0]
    part, step = rows // groups, total // groups
    factor = scale * math.log2(math.e)

    def kernel(
        q_ref, g_ref, kv_ref, kt_ref, place_ref, own_ref, begin_ref, log_ref, *refs
    ):
        dq_ref, dkv_ref, acc_ref = refs[len(done) :]
        for j in reversed(range(groups)):
            n, row = step * (j + 1), slice(j, j + 1)
            queries = per_head(q_ref, part * j, part)
            grads = per_head(g_ref, part * j, part)
            scores = masked_scores(
                kv_ref[:n, :LANES],
                queries,
                place_ref[:n, :],
                own_ref[row, :],
                begin_ref[row, :],
                step,
            )
            prob = jnp.exp2(scores * factor - log_ref[row, :])
            dprob = dot_wide(kv_ref[:n, LANES:], grads)
            inner = jnp.sum(prob * dprob, axis=0, keepdims=True)
            dscores = (prob * (dprob - inner)).astype(BF)
            dq = jnp.dot(kt_ref[:, :n], dscores, preferred_element_type=F32).T * scale
            for k in range(width // LANES):
                dq_ref[part * j : part * (j + 1), k * LANES : (k + 1) * LANES] = dq[
                    part * k : part * (k + 1)
                ].astype(BF)
            dkeys = jnp.dot(dscores, queries, preferred_element_type=F32)
            dvalues = jnp.dot(prob.astype(BF), grads, preferred_element_type=F32)
            if j == groups - 1:
                acc_ref[:, :LANES] = dkeys
                acc_ref[:, LANES:] = dvalues
            else:
                acc_ref[:n, :LANES] += dkeys
                acc_ref[:n, LANES:] += dvalues
        dkv_ref[:, :LANES] = (acc_ref[:, :LANES] * scale).astype(BF)
        dkv_ref[:, LANES:] = acc_ref[:, LANES:].astype(BF)

    return pl.pallas_call(
        kernel,
        in_specs=[pl.BlockSpec(memory_space=pltpu.VMEM)] * 8
        + [pl.BlockSpec(memory_space=pl.ANY)] * len(done),
        out_shape=[
            jax.ShapeDtypeStruct((rows, width), BF),
            jax.ShapeDtypeStruct(kv.shape, BF),
        ],
        scratch_shapes=[pltpu.VMEM(kv.shape, F32)],
        compiler_params=pltpu.CompilerParams(vmem_limit_bytes=48 * 2**20),
        cost_estimate=COST,
        name="attend_back",
    )(q, grad, kv, keys_t, places, own, begin, logs, *done)


def feed_forward(h, dy, w_fc, b_fc, w_proj, parts):
    tokens, width = h.shape
    units, part, rows = w_fc.shape[1], 512, tokens // parts
    curve = math.sqrt(2.0 / math.pi)

    def kernel(h_ref, dy_ref, fc_ref, b_ref, proj_ref, *refs):
        g_ref, du_ref, sum_ref, *dh_refs, acc_ref = refs
        step = pl.program_id(0)
        u = jnp.dot(h_ref[...], fc_ref[...], preferred_element_type=F32) + b_ref[...]
        dg = dot_wide(dy_ref[...], proj_ref[...])
        square = u * u
        bend = jnp.tanh(curve * u * (1.0 + 0.044715 * square))
        half = 0.5 + 0.5 * bend
        g_ref[...] = (u * half).astype(BF)
        slope = half + 0.5 * curve * u * (1.0 - bend * bend) * (1.0 + 3 * 0.044715 * square)
        du = (dg * slope).astype(BF)
        du_ref[...] = du
        sum_ref[...] = jnp.sum(du.astype(F32), axis=0, keepdims=True)
        term = dot_wide(du, fc_ref[...])

        @pl.when(step == 0)
        def _():
            acc_ref[...] = term

        @pl.when(step > 0)
        def _():
            acc_ref[...] += term

        @pl.when(step == units // part - 1)
        def _():
            for k, dh_ref in enumerate(dh_refs):
                dh_ref[...] = acc_ref[k * rows : (k + 1) * rows, :].astype(BF)

    along = lambda k: (0, k)
    return pl.pallas_call(
        kernel,
        grid=(units // part,),
        in_specs=[
            whole(tokens, width),
            whole(tokens, width),
            pl.BlockSpec((width, part), along),
            pl.BlockSpec((1, part), along),
            pl.BlockSpec((part, width), lambda k: (k, 0)),
        ],
        out_specs=[
            pl.BlockSpec((tokens, part), along),
            pl.BlockSpec((tokens, part), along),
            pl.BlockSpec((1, part), along),
            *[whole(rows, width)] * parts,
        ],
        out_shape=[
            jax.ShapeDtypeStruct((tokens, units), BF),
            jax.ShapeDtypeStruct((tokens, units), BF),
            jax.ShapeDtypeStruct((1, units), F32),
            *[jax.ShapeDtypeStruct((rows, width), BF)] * parts,
        ],
        scratch_shapes=[pltpu.VMEM((tokens, width), F32)],
        compiler_params=pltpu.CompilerParams(vmem_limit_bytes=56 * 2**20),
        cost_estimate=COST,
        name="feed_forward",
    )(h, dy, w_fc, b_fc.reshape(1, units), w_proj)


def products(pairs, at_left, at_right, extra=None, split=False):
    outs, per = len(at_left), len(at_left[0])
    tokens = pairs[0][0].shape[0]
    widths = [w for _, _, w in pairs]
    n, total = len(pairs), sum(widths)
    rows = per * LANES

    def kernel(at_ref, *refs):
        values, start = [], 0
        for i, width in enumerate(widths):
            own = refs[i * (per + 1) : (i + 1) * (per + 1)]
            left = jnp.concatenate([r[...] for r in own[:per]], axis=1)
            value = lax.dot_general(
                left, own[per][...], (((0,), (0,)), ((), ())), preferred_element_type=F32
            )
            if extra is not None:
                value = value + refs[n * (per + 1)][:, start : start + width].astype(F32)
            values.append(value.astype(BF))
            start += width

        def write(out):
            start = 0
            for value, width in zip(values, widths):
                out[:, start : start + width] = value
                start += width

        for k, out in enumerate(refs[n * (per + 1) + (extra is not None) :]):
            if split:
                pl.when(pl.program_id(0) == k)(functools.partial(write, out))
            else:
                write(out)

    def left_block(j):
        return lambda k, at: (0, at[k * per + j])

    def right_block(k, at):
        return (0, at[outs * per + k])

    specs, operands = [], []
    for left, right, width in pairs:
        specs += [pl.BlockSpec((tokens, LANES), left_block(j)) for j in range(per)]
        specs.append(pl.BlockSpec((tokens, width), right_block))
        operands += [left] * per + [right]
    if extra is not None:
        specs.append(pl.BlockSpec((rows, total), lambda k, at: (k, 0)))
        operands.append(extra)
    if split:
        out_specs = [whole(rows, total)] * outs
        out_shape = [jax.ShapeDtypeStruct((rows, total), BF)] * outs
    else:
        out_specs = [pl.BlockSpec((rows, total), lambda k, at: (k, 0))]
        out_shape = [jax.ShapeDtypeStruct((outs * rows, total), BF)]
    return pl.pallas_call(
        kernel,
        grid_spec=pltpu.PrefetchScalarGridSpec(
            num_scalar_prefetch=1, grid=(outs,), in_specs=specs, out_specs=out_specs
        ),
        out_shape=out_shape,
        compiler_params=pltpu.CompilerParams(vmem_limit_bytes=56 * 2**20),
        cost_estimate=COST,
        name="products",
    )(numbers([i for row in at_left for i in row] + list(at_right)), *operands)


def norm_parts(values):
    centered = values - jnp.mean(values, axis=-1, keepdims=True)
    rate = lax.rsqrt(jnp.mean(centered * centered, axis=-1, keepdims=True) + EPSILON)
    return centered * rate, rate


def norm_back(grad, gain, hat, rate):
    e = grad * gain
    inner = jnp.mean(e * hat, axis=-1, keepdims=True)
    return rate * (e - jnp.mean(e, axis=-1, keepdims=True) - hat * inner)


def shards(
    hidden,
    cotangent,
    lengths,
    source_pos,
    owner_slot,
    ln1_gain,
    ln1_bias,
    query_weight,
    query_bias,
    kv_weight,
    value_bias,
    out_weight,
    out_bias,
    ln2_gain,
    ln2_bias,
    fc_weight,
    fc_bias,
    proj_weight,
    proj_bias,
):
    rows, width = hidden.shape
    ny, nz, nctx = lax.axis_size(Y), lax.axis_size(Z), lax.axis_size(CONTEXT)
    y, xl, z, c = (lax.axis_index(a) for a in (Y, XL, Z, CORE))
    xo, co = 1 - xl, 1 - c
    ctx = lax.axis_index(CONTEXT)
    sub = rows // nctx
    head = kv_weight.shape[1] // 2
    heads = width // head
    scale = 1.0 / math.sqrt(head)
    shard = query_weight.shape[0]
    nzx = lax.axis_size(ZX)
    half = shard // 2
    ff = proj_weight.shape[0]
    block = 2 * ff

    small = jnp.concatenate(
        [
            jnp.stack([ln1_gain, ln1_bias, query_bias, out_bias, ln2_gain, ln2_bias, proj_bias]),
            jnp.pad(value_bias, (0, shard - value_bias.shape[0]))[None],
            fc_bias.reshape(-1, shard),
            jnp.zeros((4, shard), BF),
        ]
    )
    first = pack(
        [small, kv_weight],
        [out_weight, fc_weight],
        [lambda k: (c, z), lambda k: (c, k // 2 * nz + z)],
    )
    first = lax.all_to_all(first, FSDP, 0, 0, tiled=True)
    small = first[:, :16]
    gain1, bias1, bq, bo, gain2, bias2, bproj = (
        small[:, k].reshape(width).astype(F32) for k in range(7)
    )
    bv = small[:, 7, : value_bias.shape[0]].reshape(head).astype(F32)
    bfc = pick(small[:, 8:12].reshape(ny, block), y, 0).astype(F32)
    wkv = first[:, 16 : 16 + shard].reshape(width, 2 * head)

    q_mine = lax.all_to_all(
        repeat_block(query_weight, c, 2 * ny, (first,)), FSDP, 0, 0, tiled=True
    )

    def quarters(piece):
        return [piece] + [shift(piece, Z, d) for d in range(1, nz)]

    def whole_weight(mine, theirs, cost):
        there = [(z - d) % nz for d in range(nz)]
        return assemble_quarters(
            mine + theirs, [(c, k) for k in there] + [(co, k) for k in there], cost
        )

    at = 16 + shard
    o_mine = quarters(first[:, at : at + shard])

    x = hidden.astype(F32)
    hat1, rate1 = norm_parts(x)
    h1 = (hat1 * gain1 + bias1).astype(BF)
    kv = matmul(h1, wkv) + jnp.concatenate([jnp.zeros((head,), F32), bv])
    owned = lax.dynamic_slice_in_dim(owner_slot[0], ctx * rows, rows)
    target = owned // rows * sub + owned % rows - ctx * sub
    deal = (target[:, None] == jnp.arange(rows, dtype=jnp.int32)[None, :]).astype(BF)

    def dealt(array):
        pieces = array.astype(BF).reshape(nctx, sub, width)
        return lax.all_to_all(pieces, CONTEXT, 0, 0, tiled=True).reshape(rows, width)

    dealing = tall(deal, cotangent).astype(BF).reshape(nctx, -1, 2 * head)
    kv, q_mine, o_mine, dealing = gate((kv.astype(BF), q_mine, o_mine, dealing))
    q_theirs, o_theirs = swap(q_mine, CORE), [swap(m, CORE) for m in o_mine]
    kv = jnp.broadcast_to(kv[None], (nctx, rows, 2 * head))
    all_kv = lax.all_to_all(jnp.concatenate([kv, dealing], axis=1), CONTEXT, 0, 0, tiled=True)
    shards_at = [shard * k for k in range(2 * ny)]
    wq = assemble(
        [
            (q_mine, 0, [a + half * c for a in shards_at]),
            (q_theirs, 0, [a + half * co for a in shards_at]),
        ],
        width,
        width,
    )
    all_kv, wq, o_mine, o_theirs, proj_weight, first = gate(
        (all_kv, wq, o_mine, o_theirs, proj_weight, first)
    )
    dy = all_kv[:, rows:].reshape(rows, width)
    all_kv = all_kv[:, :rows]
    f_mine = quarters(first[:, at + shard :])
    p_mine = swap(lax.dynamic_slice_in_dim(proj_weight, ff // 2 * c, ff // 2), XL)
    wo = whole_weight(o_mine, o_theirs, BRIEF)
    q = (matmul(h1, wq) + bq).astype(BF)

    positions = source_pos[0]
    starts = jnp.cumsum(lengths[0]) - lengths[0]
    own_pos = lax.dynamic_slice_in_dim(positions, ctx * rows, rows)
    seq_start = jnp.max(jnp.where(starts[None, :] <= own_pos[:, None], starts[None, :], 0), axis=1)
    groups = rows // 16
    natural = jnp.moveaxis(all_kv.reshape(nctx, nctx, sub, 2 * head), 0, 1)
    natural = natural.reshape(nctx * rows, 2 * head)
    xh = lax.axis_index(XH)
    places = jnp.moveaxis(positions.reshape(nctx, nctx, sub), 0, 1).reshape(nctx * rows, 1)
    places = jnp.broadcast_to(places, (nctx * rows, LANES))

    def for_heads(array):
        array = jnp.broadcast_to(array.reshape(groups, 1, 16), (groups, heads, 16))
        return array.reshape(groups, heads * 16)

    own, begin = for_heads(own_pos), for_heads(seq_start)
    attended, logs, tops = attend(
        q, natural, natural[:, head:].T, places, own, begin, scale
    )
    local_max = jnp.max(tops.reshape(groups, heads, 16), axis=(0, 2)) * scale

    def pieces_of(array):
        return [array] + [shift(array, Y, d) for d in range(1, ny)]

    dy_pieces = pieces_of(dy)
    attended, wo, f_mine, dy_pieces, p_mine = gate((attended, wo, f_mine, dy_pieces, p_mine))
    x2 = x + matmul(attended, wo) + bo
    hat2, rate2 = norm_parts(x2)
    h2 = (hat2 * gain2 + bias2).astype(BF)

    def over_y(array):
        return jnp.concatenate(pieces_of(array))

    h2, f_mine, p_mine = gate((h2, f_mine, p_mine))
    dy_all = jnp.concatenate(dy_pieces)
    h2_pieces = pieces_of(h2)
    wfc = whole_weight(f_mine, [swap(m, CORE) for m in f_mine], COST)
    p_theirs = swap(p_mine, CORE)
    wproj = assemble(
        [
            (proj_weight, 0, [ff * xl + LANES * k for k in range(ff // LANES)]),
            (p_mine, 0, [ff * xo + ff // 2 * c + LANES * k for k in range(ff // 2 // LANES)]),
            (p_theirs, 0, [ff * xo + ff // 2 * co + LANES * k for k in range(ff // 2 // LANES)]),
        ],
        block,
        width,
    )
    h2_pieces, wfc, wproj = gate((h2_pieces, wfc, wproj))
    h2_all = jnp.concatenate(h2_pieces)
    g, du, du_sum, *dh2 = feed_forward(h2_all, dy_all, wfc, bfc, wproj, ny)

    x_ring = [(a, b) for a in (0, 1) for b in (0, 1)]
    zs = [(z + d) % nz for d in range(nz)]
    part_z = half // nz

    def flip(array, a, b):
        moves = [(2 * i + j, 2 * (i ^ a) + (j ^ b)) for i in (0, 1) for j in (0, 1)]
        return lax.ppermute(array, (XL, XH), moves)

    def over_x(parts):
        return [parts[0]] + [flip(p, a, b) for p, (a, b) in zip(parts[1:], x_ring[1:])]

    def over_z(parts):
        return [parts[0]] + [shift(parts[d], Z, d) for d in range(1, nz)]

    def core_summed(pairs, left_at, right_at):
        (theirs,) = products(pairs, left_at(co), right_at)
        return products(pairs, left_at(c), right_at, swap(theirs, CORE), True)

    dproj = core_summed(
        [(g, dy_all, width)],
        lambda core: [[(k * 2 + core) * nz + there for k in (0, 1)] for there in zs],
        [0] * nz,
    )
    dh2 = [dh2[0]] + [shift(dh2[d], Y, -d) for d in range(1, ny)]
    dh2, dproj, attended, h1 = gate((dh2, dproj, attended, h1))
    dproj = over_z(dproj)
    sent = side_by_side([], [attended, h1], [(y + d) % ny for d in range(ny)])
    sent = [sent[0]] + [shift(sent[d], Y, d) for d in range(1, ny)]
    dh2 = functools.reduce(jnp.add, [t.astype(F32) for t in dh2])

    dy_f = dy.astype(F32)
    dx2 = dy_f + norm_back(dh2, gain2, hat2, rate2)
    da = dx2.astype(BF)

    dattended = wide(da, wo).astype(BF)
    dq, dkv = attend_back(
        q, dattended, natural, natural[:, :head].T, places, own, begin, logs, scale
    )
    dfc = core_summed(
        [(h2_all, du, block // 2)],
        lambda core: [[(k * 2 + (xl ^ a)) * 2 + core for k in range(ny)] for a, _ in x_ring],
        [xh ^ b for _, b in x_ring],
    )
    dq, dkv, da, dproj, dfc, g, sent = gate((dq, dkv, da, dproj, dfc, g, sent))
    dfc = over_x(dfc)
    sent = jnp.concatenate(sent)
    attended_columns, h1_columns = sent[:, : block // ny], sent[:, block // ny :]
    dkv = jnp.moveaxis(dkv.reshape(nctx, nz, 2, 2, sub, 2 * head), 0, 3)
    dkv = dkv.reshape(nz, 2, 2, rows, 2 * head)

    def plus(mine, *got):
        return functools.reduce(jnp.add, [t.astype(F32) for t in (mine, *got)]).astype(BF)

    dkv = plus(pick(dkv, c, 2), swap(pick(dkv, co, 2), CORE))
    dkv = plus(pick(dkv, xh, 1), swap(pick(dkv, 1 - xh, 1), XH))
    dkv = plus(pick(dkv, z, 0), *[shift(pick(dkv, k, 0), Z, d) for d, k in list(enumerate(zs))[1:]])
    da_dq = over_y(jnp.concatenate([da, dq], axis=1))
    result_terms = matmul(g, wproj).astype(BF)

    dproj, dfc, da_dq, dkv, result_terms, dq = gate(
        (dproj, dfc, da_dq, dkv, result_terms, dq)
    )
    dh1 = wide(dq, wq)
    dproj = add_cut(
        dproj,
        (2, 2, half // 2, width),
        (1, 1, half // 2, width),
        [(xl ^ a, xh ^ b, 0, 0) for a, b in x_ring],
    )
    dproj = over_x(dproj)
    dfc = add_cut(
        dfc,
        (ny, nz, part_z, block // 2),
        (ny, 1, part_z, block // 2),
        [(0, there, 0, 0) for there in zs],
    )
    dfc = over_z(dfc)
    dkv_all = over_y(dkv)
    part_fc = half // nzx

    def spread(terms):
        terms = terms.reshape(2 * nzx, part_fc, -1)
        return lax.all_to_all(terms, (XL,) + ZX, 0, 0, tiled=True)

    da_all, dq_all = da_dq[:, :width], da_dq[:, width:]
    (theirs,) = products([(attended_columns, da_all, width)], [[co, 2 + co]], [0])
    (dwo,) = products(
        [(attended_columns, da_all, width)], [[c, 2 + c]], [0], swap(theirs, CORE)
    )
    dwo = spread(dwo)
    result = result_terms.reshape(ny, rows, width)
    result = [result[0]] + [shift(result[d], Y, -d) for d in range(1, ny)]
    dproj, dfc, dkv_all, result, dh1, dwo = gate((dproj, dfc, dkv_all, result, dh1, dwo))
    dproj = add_cut(
        dproj,
        (half // 2, width),
        (half // 2, width // 2),
        [(0, 0), (0, 1)],
    )
    dproj = jnp.concatenate(dproj)
    dproj_other = swap(dproj, XH)
    dfc = add_cut(
        dfc,
        (ny, part_z, block // 2),
        (1, part_z, block // 2),
        [((y + d) % ny, 0, 0) for d in range(ny)],
    )
    dfc = [dfc[0]] + [shift(dfc[d], Y, d) for d in range(1, ny)]
    dfc, dproj, dproj_other = gate((dfc, dproj, dproj_other))
    dfc = jnp.stack(dfc)

    dfc = jnp.concatenate([pick(dfc, (y - k) % ny, 0)[0] for k in range(ny)])
    there = [(z - d) % nz for d in range(nz)]
    dfc = [dfc] + [shift(dfc, Z, d) for d in range(1, nz)]
    pairs = [(h1_columns, dq_all, width), (h1_columns, dkv_all, 2 * head)]
    (theirs,) = products(pairs, [[co, 2 + co]], [0])
    (dwq,) = products(pairs, [[c, 2 + c]], [0], swap(theirs, CORE))
    dh1 = dh1 + wide(dkv, wkv)
    grad_hidden = (dx2 + norm_back(dh1, gain1, hat1, rate1)).astype(BF)
    result = functools.reduce(jnp.add, [t.astype(F32) for t in result])
    result = dealt((x2 + result + bproj).astype(BF))
    def total(array):
        return jnp.sum(array.astype(F32), axis=0)

    vectors = [
        total(dy),
        total(dh2 * hat2),
        total(dh2),
        total(da),
        total(dq),
        total(dh1 * hat1),
        total(dh1),
    ]
    vectors = [v.reshape(2 * ny, 1, shard) for v in vectors]
    du_sum = du_sum.reshape(1, 2, ff // shard, shard)
    du_sum = lax.dynamic_update_slice(
        jnp.zeros((ny, 2, ff // shard, shard), F32), du_sum, (y, 0, 0, 0)
    )
    bv_sum = total(dkv[:, head:]).reshape(2 * ny, 1, -1)
    top_high = lax.reduce_precision(local_max, 8, 7)
    tops = jnp.concatenate([top_high, local_max - top_high])
    tops = jnp.broadcast_to(tops, (2 * ny, 1, 2 * heads))
    last = [jnp.pad(v, ((0, 0), (0, 0), (0, shard - v.shape[2]))) for v in (bv_sum, tops)]
    vectors += [du_sum.reshape(2 * ny, -1, shard), *last]
    joined = jnp.concatenate(vectors, axis=1).astype(BF)
    joined = jnp.pad(joined, ((0, 0), (0, 16 - joined.shape[1]), (0, 0)))
    joined = jnp.broadcast_to(joined[:, None], (2 * ny, nctx, *joined.shape[1:]))
    joined = joined.reshape(-1, 16, shard)
    joined = lax.all_to_all(joined, EVERY, 0, 0, tiled=True)
    dfc, dwq, dwo, dproj, dproj_other, result, joined = gate(
        (dfc, dwq, dwo, dproj, dproj_other, result, joined)
    )
    output = matmul(deal, result).astype(BF)

    dfc = jnp.stack(dfc)
    dfc_other = swap(dfc, XH)
    dproj = pair(dproj, dproj_other, xh)
    dproj = [dproj] + [shift(dproj, Z, d) for d in range(1, nz)]
    small_w = jnp.concatenate([dwo, spread(dwq)], axis=2)
    dfc, dfc_other, dproj, small_w = gate((dfc, dfc_other, dproj, small_w))
    small_w = copies(jnp.sum(small_w.astype(F32), axis=0).astype(BF), ZX)
    dfc = pair(dfc, dfc_other, xh)
    mine = [dfc] + dproj
    mine = mine + [swap(m, CORE) for m in mine]
    grad_proj_w, grad_fc_w = lay_both(
        mine,
        [c * nz + k for k in there] + [co * nz + k for k in there],
        half,
        part_z,
        ny,
    )
    small_w, grad_proj_w, grad_fc_w = gate((small_w, grad_proj_w, grad_fc_w))
    grad_out_w, grad_query_w, grad_kv_w = laid_out(
        small_w,
        swap(small_w, CORE),
        c,
        [(part_fc, width), (part_fc, width), (part_fc, 2 * head)],
        lambda piece: (piece[:, :width], piece[:, width : 2 * width], piece[:, 2 * width :]),
    )

    tops = joined[:, 12].astype(F32)
    maxima = jnp.max(tops[:, :heads] + tops[:, heads : 2 * heads], axis=0)
    joined = jnp.sum(joined.astype(F32), axis=0)
    g_bproj, g_gain2, g_bias2, g_bo, g_bq, g_gain1, g_bias1 = (joined[k] for k in range(7))
    g_bfc, g_bv = joined[7:11].reshape(ff), joined[11, : value_bias.shape[0]]

    clip_ratio = CLIP_LIMIT / jnp.maximum(maxima, CLIP_LIMIT)
    column_scale = jnp.repeat(jnp.sqrt(clip_ratio), head)
    clipped_qw = query_weight.astype(F32) * column_scale[None, :]
    clipped_qb = query_bias.astype(F32) * lax.dynamic_slice_in_dim(
        column_scale, lax.axis_index(FSDP) * shard, shard
    )
    clipped_kw = kv_weight[:, :head].astype(F32) * jnp.sqrt(jnp.min(clip_ratio))
    return (
        output,
        grad_hidden,
        g_gain1,
        g_bias1,
        grad_query_w,
        g_bq,
        grad_kv_w,
        g_bv,
        grad_out_w,
        g_bo,
        g_gain2,
        g_bias2,
        grad_fc_w,
        g_bfc,
        grad_proj_w,
        g_bproj,
        maxima,
        clipped_qw,
        clipped_qb,
        clipped_kw,
    )


def solution(mesh):
    torus = Mesh(mesh.devices.reshape(4, 2, 4, 2, 2), EVERY)
    tokens, table, vector, matrix = P(EVERY, None), P(FSDP, None), P(FSDP), P(FSDP, None)
    return jax.shard_map(
        shards,
        mesh=torus,
        in_specs=(
            tokens,
            tokens,
            table,
            table,
            table,
            vector,
            vector,
            matrix,
            vector,
            matrix,
            vector,
            matrix,
            vector,
            vector,
            vector,
            matrix,
            vector,
            matrix,
            vector,
        ),
        out_specs=(
            tokens,
            tokens,
            vector,
            vector,
            matrix,
            vector,
            matrix,
            vector,
            matrix,
            vector,
            vector,
            vector,
            matrix,
            vector,
            matrix,
            vector,
            P(),
            matrix,
            vector,
            matrix,
        ),
        check_vma=False,
    )
```
